128 devices in a mesh: row: 8 (over z_lo, x), col: 16 (over y, z_hi, core).
Axes of the slice: x: 4, y: 4, z: 4 (z_hi: 2, z_lo: 2; z = z_hi * 2 + z_lo), core: 2. Of those that a mesh axis runs over, the one named last changes fastest.
Arguments:
- patches: bfloat16 [32, 256, 384], P('row', 'col'), may hold values from -6 to 6
- in_weight: bfloat16 [384, 1536], replicated, may hold values from -0.3125 to 0.3125
- conv_weight: float32 [3, 3, 768], replicated, may hold values from -2 to 2
- proj_weight: bfloat16 [4, 768, 56], replicated, may hold values from -0.21875 to 0.21875
- step_weight: bfloat16 [4, 24, 768], replicated, may hold values from -1.25 to 1.25
- step_bias: float32 [4, 768], replicated, may hold values from -6 to -2.5
- decay_rate: float32 [4, 16, 768], replicated, as said below
- skip_gain: float32 [4, 768], replicated, may hold values from 0.5 to 1.5
- out_weight: bfloat16 [768, 384], replicated, may hold values from -0.21875 to 0.21875
Outputs:
- block_out: bfloat16 [32, 256, 384], P('row', 'col')
The draws below stay inside these ranges and needn't reach their ends.
Inputs may be any that keep to these rules, and one draw needn't show every extreme that they name: `decay_rate`: positive rates of the state's decay per unit of step size.
All inputs are finite; a program needn't handle non-finite values.
Results may differ from the reference program's by a relative error of at most 0.0092.
Values may be sent and summed in bfloat16 or wider, within the bound.
A program may use at most 128 MiB of HBM per device.

```python
import math
import jax
import jax.numpy as jnp
from jax import lax

CHANNELS = 384
EXPANDED = 768
STATES = 16
STEP_RANK = 24
HEIGHT = 32
WIDTH = 256
POSITIONS = 8192


def draw_decay_rate(key, part):
    key = jax.random.fold_in(key, 7)
    exponent = 1.0
    lowest = 1.2 / POSITIONS
    fraction = jax.random.uniform(key, (4, STATES, EXPANDED), jnp.float32)
    fraction = fraction ** exponent
    rates = lowest * jnp.exp(fraction * math.log(3.0 / lowest))
    return rates.astype(jnp.float32)


def level_of(key, dims, pieces, least, largest):
    def one(axis_at, parts):
        draws = jax.random.uniform(jax.random.fold_in(jax.random.fold_in(key, 6), axis_at), (parts,), jnp.float32, least / len(pieces), largest / len(pieces))
        return jnp.repeat(jnp.exp(draws), dims[axis_at] // parts).reshape((-1,) + (1,) * (len(dims) - axis_at - 1))

    level = one(*pieces[0])
    for cut in pieces[1:]:
        level = level * one(*cut)
    return level


def noise(key, dims, scale, limit, split=(), held_as=jnp.bfloat16):
    entries = jax.random.normal(key, dims, jnp.float32) * scale
    if len(split) > 0:
        entries = level_of(key, dims, split, -0.22, 0.18) * entries
    return jnp.clip(entries, min=-limit, max=limit).astype(held_as)


def setup_inputs(seed: int = 0) -> dict:
    streams_of = jax.random.split(jax.random.key(seed), 10)
    return {
        "patches": noise(streams_of[0], (HEIGHT, WIDTH, CHANNELS), 1.0, 6.0, ((0, 8), (1, 16))),
        "in_weight": noise(streams_of[1], (CHANNELS, 2 * EXPANDED), CHANNELS ** -0.5, 0.3125),
        "conv_weight": noise(streams_of[2], (3, 3, EXPANDED), 9 ** -0.5, 2.0, (), jnp.float32),
        "proj_weight": noise(streams_of[3], (4, EXPANDED, STEP_RANK + 2 * STATES), EXPANDED ** -0.5, 0.21875),
        "step_weight": noise(streams_of[4], (4, STEP_RANK, EXPANDED), STEP_RANK ** -0.5, 1.25),
        "step_bias": jnp.clip(jax.random.uniform(streams_of[5], (4, EXPANDED), jnp.float32, -6.0, -2.5), -6.0, -2.5),
        "decay_rate": draw_decay_rate(jax.random.fold_in(streams_of[9], 71), 0),
        "skip_gain": jnp.clip(jax.random.uniform(streams_of[7], (4, EXPANDED), jnp.float32, 0.5, 1.5), 0.5, 1.5),
        "out_weight": noise(streams_of[8], (EXPANDED, CHANNELS), EXPANDED ** -0.5, 0.21875),
    }


epsilon = 1e-05

def layer_norm(values):
    average = lax.optimization_barrier(jnp.mean(values, -1, keepdims=True))
    centred = values - average
    variance = lax.optimization_barrier(jnp.mean(centred * centred, -1, keepdims=True))
    return centred * lax.rsqrt(variance + epsilon)

def order_tokens(field, branch):
    if branch % 2 == 1:
        field = jnp.swapaxes(field, 0, 1)
    field = field.reshape((POSITIONS,) + field.shape[2:])
    if branch >= 2:
        field = field[::-1]
    return field

def restore_order(field, branch):
    if branch >= 2:
        field = field[::-1]
    if branch % 2 == 1:
        return jnp.swapaxes(field.reshape(WIDTH, HEIGHT, -1), 0, 1)
    return field.reshape(HEIGHT, WIDTH, -1)

def scan_sequence(signal, step_size, write_weights, read_weights, decays, skip):

    def advance(states, inputs):
        signal_now, step_now, write_now, read_now = inputs
        states = jnp.exp(-decays * step_now[None, :]) * states + (step_now * signal_now)[None, :] * write_now[:, None]
        result = lax.optimization_barrier(jnp.sum(read_now[:, None] * states, 0)) + skip * signal_now
        return (states, result)
    initial = jnp.zeros(decays.shape, jnp.float32)
    _, outputs = lax.scan(advance, initial, (signal, step_size, write_weights, read_weights))
    return outputs

def reference(patches, in_weight, conv_weight, proj_weight, step_weight, step_bias, decay_rate, skip_gain, out_weight):
    normed = layer_norm(patches.astype(jnp.float32)).astype(jnp.bfloat16)
    projected = jnp.dot(normed.reshape(POSITIONS, CHANNELS), in_weight, preferred_element_type=jnp.float32)
    conv_input = lax.optimization_barrier(projected[:, :EXPANDED].astype(jnp.bfloat16))
    gate_input = lax.optimization_barrier(projected[:, EXPANDED:].astype(jnp.bfloat16))
    padded = jnp.pad(conv_input.reshape(HEIGHT, WIDTH, EXPANDED).astype(jnp.float32), ((1, 1), (1, 1), (0, 0)))
    filtered = jnp.zeros((HEIGHT, WIDTH, EXPANDED), jnp.float32)
    for down_shift in range(3):
        for side_shift in range(3):
            filtered = filtered + padded[down_shift:down_shift + HEIGHT, side_shift:side_shift + WIDTH] * conv_weight[down_shift, side_shift]
    activated = lax.optimization_barrier(jax.nn.silu(filtered).astype(jnp.bfloat16))
    tokens = activated.reshape(POSITIONS, EXPANDED)
    signal = tokens.astype(jnp.float32).reshape(HEIGHT, WIDTH, EXPANDED)
    summed = jnp.zeros((HEIGHT, WIDTH, EXPANDED), jnp.float32)
    for branch in range(4):
        projections = lax.optimization_barrier(jnp.dot(tokens, proj_weight[branch], preferred_element_type=jnp.float32).astype(jnp.bfloat16))
        step_size = jax.nn.softplus(jnp.dot(projections[:, :STEP_RANK], step_weight[branch], preferred_element_type=jnp.float32) + step_bias[branch])
        write_weights = projections[:, STEP_RANK:STEP_RANK + STATES].astype(jnp.float32)
        read_weights = projections[:, STEP_RANK + STATES:].astype(jnp.float32)
        outputs = scan_sequence(order_tokens(signal, branch), order_tokens(step_size.reshape(HEIGHT, WIDTH, EXPANDED), branch), order_tokens(write_weights.reshape(HEIGHT, WIDTH, STATES), branch), order_tokens(read_weights.reshape(HEIGHT, WIDTH, STATES), branch), decay_rate[branch], skip_gain[branch])
        summed = summed + restore_order(outputs, branch)
    gated_out = (layer_norm(summed).reshape(POSITIONS, EXPANDED) * jax.nn.silu(gate_input.astype(jnp.float32))).astype(jnp.bfloat16)
    result = jnp.dot(gated_out, out_weight, preferred_element_type=jnp.float32).astype(jnp.bfloat16)
    return result.reshape(HEIGHT, WIDTH, CHANNELS)
```

```python
import functools

import jax
import jax.numpy as jnp
from jax import lax
from jax.experimental import pallas as pl
from jax.experimental.pallas import tpu as pltpu
from jax.sharding import PartitionSpec as P

MESH = pl.DeviceIdType.MESH
F32, BF16 = jnp.float32, jnp.bfloat16

ROWS, COLS = 8, 16
TR, TC = 4, 16
TOK = TR * TC
CH, HID = 384, 768
RANK, NS = 24, 16
KC = 8
CW = HID // KC
LANE = 128
SECOND = 64
SEG, POS = 16, 32
SPAN = SEG * POS
PEERS = 16
LOG2E = 1.4426950408889634
epsilon = 1e-05


def normalised(x):
    average = jnp.mean(x, -1, keepdims=True)
    centred = x - average
    variance = jnp.mean(centred * centred, -1, keepdims=True)
    return centred * lax.rsqrt(variance + epsilon)


def silu(v):
    return v / (1.0 + jnp.exp(-v))


def softplus(v):
    return jnp.maximum(v, 0.0) + jnp.log1p(jnp.exp(-jnp.abs(v)))


def dot(a, b):
    return jnp.dot(a, b, preferred_element_type=F32)


def lane_mask(rows):
    return lax.broadcasted_iota(jnp.int32, (rows, LANE), 1) < CW


def chunk(x, k):
    low = CW * k
    tile, off = low // LANE, low % LANE
    width = min(2 * LANE, HID - tile * LANE)
    window = x[:, tile * LANE : tile * LANE + width]
    if off:
        window = pltpu.roll(window, width - off, 1)
    return jnp.where(lane_mask(x.shape[0]), window[:, :LANE], 0.0)


def kernel(
    patches,
    in_w,
    conv_w,
    proj_w,
    step_w,
    step_b,
    decay,
    skip,
    out_w,
    out,
    halo_send,
    halo_recv,
    pad,
    gate,
    act,
    proj,
    a2a_send,
    raw,
    tokens,
    projf,
    sw,
    bias,
    dec,
    perm,
    step,
    inflow,
    hbuf,
    pbuf,
    start,
    msg,
    cbuf,
    ysum,
    ysend,
    yrecv,
    halo_ss,
    halo_rs,
    a2a_ss,
    a2a_rs,
    car_ss,
    car_rs,
    ret_ss,
    ret_rs,
):
    R = lax.axis_index("row")
    C = lax.axis_index("col")
    half = lax.rem(C, 2)
    pair = C - half + (1 - half)
    kchunk = lax.div(C, 2)

    barrier = pltpu.get_barrier_semaphore()

    def greet(r, c):
        pl.semaphore_signal(barrier, inc=1, device_id=(r, c), device_id_type=MESH)

    def row_at(o):
        return lax.rem(R + o, ROWS)

    def col_at(o):
        return lax.rem(C + o, COLS)

    for o in range(1, COLS):
        greet(R, col_at(o))
    for o in range(1, ROWS):
        greet(row_at(o), C)
        greet(row_at(o), pair)
    beside = lax.rem(C + 15 + 2 * half, COLS)
    greet(row_at(1), beside)
    greet(row_at(ROWS - 1), beside)
    pl.semaphore_wait(barrier, 15 + 7 + 7 + 2)

    x = patches[...]
    gr = lax.broadcasted_iota(jnp.int32, (32, TOK), 0)
    gt = lax.broadcasted_iota(jnp.int32, (32, TOK), 1)
    wanted = jnp.where(gr < 16, gr * TC + TC - 1, (gr - 16) * TC)
    picks = jnp.where((gt == wanted) & (lax.rem(gr, 16) < TR), 1.0, 0.0).astype(BF16)
    top, bottom = patches.at[pl.ds(0, 16)], patches.at[pl.ds(TOK - 16, 16)]
    right_edge, left_edge = halo_send.at[pl.ds(0, 16)], halo_send.at[pl.ds(16, 16)]
    rim = (
        (bottom, 1, 0),
        (top, 7, 0),
        (right_edge, 0, 1),
        (left_edge, 0, 15),
        (bottom, 1, 1),
        (bottom, 1, 15),
        (top, 7, 1),
        (top, 7, 15),
    )
    rim_copies = []
    for slot, (edge, dr, dc) in enumerate(rim):
        rim_copies.append(
            pltpu.make_async_remote_copy(
                src_ref=edge,
                dst_ref=halo_recv.at[pl.ds(slot * 16, 16)],
                send_sem=halo_ss.at[slot],
                recv_sem=halo_rs.at[slot],
                device_id=(row_at(dr), col_at(dc)),
                device_id_type=MESH,
            )
        )
    for slot in (0, 1, 4, 5, 6, 7):
        rim_copies[slot].start()
    halo_send[...] = dot(picks, x).astype(BF16)
    for slot in (2, 3):
        rim_copies[slot].start()

    normed = normalised(x.astype(F32)).astype(BF16)
    gate_in = dot(normed, in_w[:, HID:]).astype(BF16).astype(F32)
    gate_silu = silu(gate_in)
    for k in range(KC):
        gate[k] = chunk(gate_silu, k)
    own = dot(normed, in_w[:, :HID]).astype(BF16).astype(F32)
    for i in range(TR):
        pad[1 + i, 8 : 8 + TC, :] = own[i * TC : (i + 1) * TC]

    sw[...] = jnp.zeros_like(sw)
    for g in range(2):
        place = kchunk if g == 0 else R
        shift = lax.rem(HID - CW * place, HID)
        for d in range(2):
            branch = g + 2 * d

            def part(value):
                turned = pltpu.roll(value, shift, 1)[:, :LANE]
                return jnp.where(lane_mask(value.shape[0]), turned, 0.0)

            sw[g, d * SECOND : d * SECOND + RANK, d * LANE : (d + 1) * LANE] = part(
                step_w[branch].astype(F32)
            )
            bias[g, :, d * LANE : (d + 1) * LANE] = part(
                jnp.broadcast_to(step_b[branch : branch + 1, :], (8, HID))
            )
            rates = part(decay[branch]) * (-LOG2E)
            for n in range(NS):
                dec[2 * g + d, n * 8 : (n + 1) * 8, :] = jnp.broadcast_to(
                    rates[n : n + 1], (8, LANE)
                )
    po = lax.broadcasted_iota(jnp.int32, (256, 256), 0)
    pq = lax.broadcasted_iota(jnp.int32, (256, 256), 1)
    source = lax.rem(po, 8) * 32 + lax.rem(lax.div(po, 8), 2) * 16 + lax.div(po, 16)
    perm[0] = jnp.where(pq == source, 1.0, 0.0).astype(BF16)
    target = lax.rem(pq, 8) * 32 + lax.rem(lax.div(pq, 8), 2) * 16 + lax.div(pq, 16)
    perm[1] = jnp.where(po == target, 1.0, 0.0).astype(BF16)

    for slot in range(8):
        rim_copies[slot].wait_recv()
    not_first_row = jnp.where(R > 0, 1.0, 0.0)
    not_last_row = jnp.where(R < ROWS - 1, 1.0, 0.0)
    not_first_col = jnp.where(C > 0, 1.0, 0.0)
    not_last_col = jnp.where(C < COLS - 1, 1.0, 0.0)
    rim_in = dot(normalised(halo_recv[...].astype(F32)).astype(BF16), in_w[:, :HID])
    rim_in = rim_in.astype(BF16).astype(F32)
    pad[0, 8 : 8 + TC, :] = rim_in[0:16] * not_first_row
    pad[TR + 1, 8 : 8 + TC, :] = rim_in[16:32] * not_last_row
    left = rim_in[32:48] * not_first_col
    right = rim_in[48:64] * not_last_col
    for i in range(TR):
        pad[1 + i, 7:8, :] = left[i : i + 1]
        pad[1 + i, 8 + TC : 9 + TC, :] = right[i : i + 1]
    pad[0, 7:8, :] = rim_in[79:80] * (not_first_row * not_first_col)
    pad[0, 8 + TC : 9 + TC, :] = rim_in[80:81] * (not_first_row * not_last_col)
    pad[TR + 1, 7:8, :] = rim_in[111:112] * (not_last_row * not_first_col)
    pad[TR + 1, 8 + TC : 9 + TC, :] = rim_in[112:113] * (not_last_row * not_last_col)

    for i in range(TR):
        total = jnp.zeros((TC, HID), F32)
        for p in range(3):
            for q in range(3):
                total = total + pad[i + p, 7 + q : 7 + q + TC, :] * conv_w[p, q : q + 1, :]
        act[i * TC : (i + 1) * TC, :] = silu(total).astype(BF16).astype(F32)

    activated = act[...]
    low = activated.astype(BF16)
    proj[...] = jnp.zeros_like(proj)
    for branch in range(4):
        g, d = branch % 2, branch // 2
        proj[g, :, d * SECOND : d * SECOND + RANK + 2 * NS] = dot(low, proj_w[branch])
    for k in range(KC):
        part_k = chunk(activated, k).astype(BF16)
        for g in range(2):
            a2a_send[g, k, :, :LANE] = part_k
            a2a_send[g, k, :, LANE:] = proj[g].astype(BF16)

    a2a = {0: [], 1: []}
    for o in range(1, ROWS):
        peer = row_at(o)
        a2a[1].append(
            pltpu.make_async_remote_copy(
                src_ref=a2a_send.at[1, peer],
                dst_ref=tokens.at[1, pl.ds(R * TOK, TOK)],
                send_sem=a2a_ss.at[1, o],
                recv_sem=a2a_rs.at[1, o],
                device_id=(peer, C),
                device_id_type=MESH,
            )
        )
    slot = half * 8 + kchunk
    for o in range(1, COLS):
        peer = col_at(o)
        a2a[0].append(
            pltpu.make_async_remote_copy(
                src_ref=a2a_send.at[0, lax.div(peer, 2), pl.ds(lax.rem(peer, 2) * 32, 32)],
                dst_ref=raw.at[pl.ds(slot * 32, 32)],
                send_sem=a2a_ss.at[0, o],
                recv_sem=a2a_rs.at[0, o],
                device_id=(R, peer),
                device_id_type=MESH,
            )
        )
    for g in (1, 0):
        for copy in a2a[g]:
            copy.start()
    tokens[1, pl.ds(R * TOK, TOK), :] = a2a_send[1, R]
    raw[pl.ds(slot * 32, 32), :] = a2a_send[0, kchunk, pl.ds(half * 32, 32), :]

    place = (R * 2 + half, C)

    def peer_of(g, s):
        if g == 0:
            return (lax.div(s, 2), C - half + lax.rem(s, 2))
        return (R, s)

    carries = {0: [], 1: []}
    for g in range(2):
        for o in range(1, PEERS):
            s = lax.rem(place[g] + o, PEERS)
            way = jnp.where(s > place[g], 0, 1)
            carries[g].append(
                pltpu.make_async_remote_copy(
                    src_ref=msg.at[g, way],
                    dst_ref=cbuf.at[g, place[g]],
                    send_sem=car_ss.at[g, o],
                    recv_sem=car_rs.at[g, o],
                    device_id=peer_of(g, s),
                    device_id_type=MESH,
                )
            )

    def first_pass(g):
        lines = tokens[g].astype(F32)
        projf[g] = lines[:, LANE:]
        raw_step = dot(tokens[g, :, LANE:], sw[g].astype(BF16)) + bias[g, 0:1, :]
        steps = softplus(raw_step)
        for d in range(2):
            one = steps[:, d * LANE : (d + 1) * LANE]
            step[2 * g + d] = one
            inflow[2 * g + d] = one * lines[:, :LANE]
        for d in range(2):
            b = 2 * g + d
            for hf in range(2):

                def body(i, carry):
                    held, decayed = carry
                    pos = POS - 1 - i if d == 1 else i
                    row = pl.multiple_of(pos * SEG + hf * 8, 8)
                    st = step[b, pl.ds(row, 8), :]
                    fl = inflow[b, pl.ds(row, 8), :]
                    pj = projf[g, pl.ds(row, 8), :]
                    new_held, new_decayed = [], []
                    for n in range(NS):
                        a = jnp.exp2(st * dec[b, n * 8 : (n + 1) * 8, :])
                        lane = d * SECOND + RANK + n
                        w = jnp.broadcast_to(pj[:, lane : lane + 1], (8, LANE))
                        h = a * held[n] + fl * w
                        q = a * decayed[n]
                        at = pl.multiple_of((pos * NS + n) * SEG + hf * 8, 8)
                        hbuf[b, pl.ds(at, 8), :] = h
                        pbuf[b, pl.ds(at, 8), :] = q
                        new_held.append(h)
                        new_decayed.append(q)
                    return tuple(new_held), tuple(new_decayed)

                zero = jnp.zeros((8, LANE), F32)
                lax.fori_loop(
                    0,
                    POS,
                    body,
                    (tuple(zero for _ in range(NS)), tuple(zero + 1.0 for _ in range(NS))),
                )
            last = 0 if d == 1 else (POS - 1) * NS * SEG
            held = jnp.zeros((NS, LANE), F32)
            decayed = jnp.ones((NS, LANE), F32)
            for t in range(SEG):
                seg = SEG - 1 - t if d == 1 else t
                a = pbuf[b, pl.ds(last + seg, NS, stride=SEG), :]
                held = a * held + hbuf[b, pl.ds(last + seg, NS, stride=SEG), :]
                decayed = a * decayed
            msg[g, d, :NS, :] = held
            msg[g, d, NS:, :] = decayed
        for copy in carries[g]:
            copy.start()

    def second_pass(g):
        for d in range(2):
            b = 2 * g + d
            held = jnp.zeros((NS, LANE), F32)
            for t in range(PEERS):
                s = PEERS - 1 - t if d == 1 else t
                ahead = s > place[g] if d == 1 else s < place[g]
                later = cbuf[g, s, NS:, :] * held + cbuf[g, s, :NS, :]
                held = jnp.where(ahead, later, held)
            last = 0 if d == 1 else (POS - 1) * NS * SEG
            for t in range(SEG):
                seg = SEG - 1 - t if d == 1 else t
                start[b, pl.ds(seg, NS, stride=SEG), :] = held
                held = (
                    pbuf[b, pl.ds(last + seg, NS, stride=SEG), :] * held
                    + hbuf[b, pl.ds(last + seg, NS, stride=SEG), :]
                )
        for hf in range(2):

            def body(pos, carry):
                row = pl.multiple_of(pos * SEG + hf * 8, 8)
                pj = projf[g, pl.ds(row, 8), :]
                total = jnp.zeros((8, LANE), F32)
                for d in range(2):
                    b = 2 * g + d
                    for n in range(NS):
                        at = pl.multiple_of((pos * NS + n) * SEG + hf * 8, 8)
                        h = (
                            hbuf[b, pl.ds(at, 8), :]
                            + pbuf[b, pl.ds(at, 8), :] * start[b, n * SEG + hf * 8 : n * SEG + hf * 8 + 8, :]
                        )
                        lane = d * SECOND + RANK + NS + n
                        r = jnp.broadcast_to(pj[:, lane : lane + 1], (8, LANE))
                        total = total + r * h
                ysum[g, pl.ds(row, 8), :] = total
                return carry

            lax.fori_loop(0, POS, body, 0)

    for g in range(2):
        cbuf[g, place[g]] = jnp.zeros((2 * NS, LANE), F32)
    for copy in a2a[1]:
        copy.wait_recv()
    first_pass(1)
    for copy in a2a[0]:
        copy.wait_recv()
    for b in range(2):
        tokens[0, b * 256 : (b + 1) * 256, :] = dot(
            perm[0], raw[b * 256 : (b + 1) * 256, :]
        ).astype(BF16)
    first_pass(0)

    returns = {0: [], 1: []}
    for o in range(1, ROWS):
        peer = row_at(o)
        returns[1].append(
            pltpu.make_async_remote_copy(
                src_ref=ysend.at[1, pl.ds(peer * TOK, TOK)],
                dst_ref=yrecv.at[1, R],
                send_sem=ret_ss.at[1, o],
                recv_sem=ret_rs.at[1, o],
                device_id=(peer, C),
                device_id_type=MESH,
            )
        )
    for o in range(1, COLS):
        peer = col_at(o)
        at = lax.rem(peer, 2) * 8 + lax.div(peer, 2)
        returns[0].append(
            pltpu.make_async_remote_copy(
                src_ref=ysend.at[0, pl.ds(at * 32, 32)],
                dst_ref=yrecv.at[0, kchunk, pl.ds(half * 32, 32)],
                send_sem=ret_ss.at[0, o],
                recv_sem=ret_rs.at[0, o],
                device_id=(R, peer),
                device_id_type=MESH,
            )
        )

    for copy in carries[1]:
        copy.wait_recv()
    second_pass(1)
    ysend[1] = ysum[1].astype(BF16)
    for copy in returns[1]:
        copy.start()
    yrecv[1, R] = ysend[1, pl.ds(R * TOK, TOK), :]

    for copy in carries[0]:
        copy.wait_recv()
    second_pass(0)
    for b in range(2):
        ysend[0, b * 256 : (b + 1) * 256, :] = dot(
            perm[1], ysum[0, b * 256 : (b + 1) * 256, :].astype(BF16)
        ).astype(BF16)
    for copy in returns[0]:
        copy.start()
    yrecv[0, kchunk, pl.ds(half * 32, 32), :] = ysend[0, pl.ds(slot * 32, 32), :]

    gains = skip[0:1, :] + skip[1:2, :] + skip[2:3, :] + skip[3:4, :]
    skipped = act[...] * gains
    pieces = [chunk(skipped, k) for k in range(KC)]
    for g in (1, 0):
        for copy in returns[g]:
            copy.wait_recv()
    pieces = [
        pieces[k] + yrecv[0, k].astype(F32) + yrecv[1, k].astype(F32) for k in range(KC)
    ]
    average = sum(jnp.sum(z, -1, keepdims=True) for z in pieces) * (1.0 / HID)
    mask = lane_mask(TOK)
    centred = [jnp.where(mask, z - average, 0.0) for z in pieces]
    variance = sum(jnp.sum(z * z, -1, keepdims=True) for z in centred) * (1.0 / HID)
    scale = lax.rsqrt(variance + epsilon)
    result = jnp.zeros((TOK, CH), F32)
    for k in range(KC):
        gated = (centred[k] * scale * gate[k]).astype(BF16)
        result = result + dot(gated[:, :CW], out_w[k * CW : (k + 1) * CW, :])
    out[...] = result.astype(BF16)

    for copy in rim_copies:
        copy.wait_send()
    for g in range(2):
        for group in (a2a[g], carries[g], returns[g]):
            for copy in group:
                copy.wait_send()


def per_device(
    patches,
    in_weight,
    conv_weight,
    proj_weight,
    step_weight,
    step_bias,
    decay_rate,
    skip_gain,
    out_weight,
):
    vmem = pl.BlockSpec(memory_space=pltpu.VMEM)
    dma = pltpu.SemaphoreType.DMA
    result = pl.pallas_call(
        kernel,
        out_shape=jax.ShapeDtypeStruct((TOK, CH), BF16),
        in_specs=[vmem] * 9,
        out_specs=vmem,
        scratch_shapes=[
            pltpu.VMEM((32, CH), BF16),
            pltpu.VMEM((128, CH), BF16),
            pltpu.VMEM((TR + 2, 32, HID), F32),
            pltpu.VMEM((KC, TOK, LANE), F32),
            pltpu.VMEM((TOK, HID), F32),
            pltpu.VMEM((2, TOK, LANE), F32),
            pltpu.VMEM((2, KC, TOK, 2 * LANE), BF16),
            pltpu.VMEM((SPAN, 2 * LANE), BF16),
            pltpu.VMEM((2, SPAN, 2 * LANE), BF16),
            pltpu.VMEM((2, SPAN, LANE), F32),
            pltpu.VMEM((2, LANE, 2 * LANE), F32),
            pltpu.VMEM((2, 8, 2 * LANE), F32),
            pltpu.VMEM((4, NS * 8, LANE), F32),
            pltpu.VMEM((2, 256, 256), BF16),
            pltpu.VMEM((4, SPAN, LANE), F32),
            pltpu.VMEM((4, SPAN, LANE), F32),
            pltpu.VMEM((4, SPAN * NS, LANE), F32),
            pltpu.VMEM((4, SPAN * NS, LANE), F32),
            pltpu.VMEM((4, NS * SEG, LANE), F32),
            pltpu.VMEM((2, 2, 2 * NS, LANE), F32),
            pltpu.VMEM((2, PEERS, 2 * NS, LANE), F32),
            pltpu.VMEM((2, SPAN, LANE), F32),
            pltpu.VMEM((2, SPAN, LANE), BF16),
            pltpu.VMEM((2, KC, TOK, LANE), BF16),
            dma((8,)),
            dma((8,)),
            dma((2, 16)),
            dma((2, 16)),
            dma((2, 16)),
            dma((2, 16)),
            dma((2, 16)),
            dma((2, 16)),
        ],
        compiler_params=pltpu.CompilerParams(
            collective_id=0, has_side_effects=True, vmem_limit_bytes=60 * 1024 * 1024
        ),
        name="ss2d",
    )(
        patches.reshape(TOK, CH),
        in_weight,
        conv_weight,
        proj_weight,
        step_weight,
        step_bias,
        decay_rate,
        skip_gain,
        out_weight,
    )
    return result.reshape(TR, TC, CH)


def solution(mesh):
    return jax.shard_map(
        per_device,
        mesh=mesh,
        in_specs=(P("row", "col", None), P(), P(), P(), P(), P(), P(), P(), P()),
        out_specs=P("row", "col", None),
        check_vma=False,
    )
```

```python
import functools

import jax
import jax.numpy as jnp
from jax import lax
from jax.experimental import pallas as pl
from jax.experimental.pallas import tpu as pltpu
from jax.sharding import PartitionSpec as P

MESH = pl.DeviceIdType.MESH
F32, BF16 = jnp.float32, jnp.bfloat16

ROWS, COLS = 8, 16
TR, TC = 4, 16
TOK = TR * TC
CH, HID = 384, 768
RANK, NS = 24, 16
KC = 8
CW = HID // KC
LANE = 128
SECOND = 64
SEG, POS = 16, 32
KIND = 3
QUAD = KIND * LANE
SLOT = NS // 4 * KIND
STATE = SLOT * LANE
MAP = 16
SPAN = SEG * POS
PEERS = 16
LOG2E = 1.4426950408889634
epsilon = 1e-05


def normalised(x):
    average = jnp.mean(x, -1, keepdims=True)
    centred = x - average
    variance = jnp.mean(centred * centred, -1, keepdims=True)
    return centred * lax.rsqrt(variance + epsilon)


def silu(v):
    return v / (1.0 + jnp.exp(-v))


def softplus(v):
    return jnp.maximum(v, 0.0) + jnp.log1p(jnp.exp(-jnp.abs(v)))


def dot(a, b):
    return jnp.dot(a, b, preferred_element_type=F32)


def two_parts(x):
    high = x.astype(BF16)
    return jnp.concatenate([high, (x - high.astype(F32)).astype(BF16)], axis=1)


def zero_one(shape, test):
    one = lax.broadcasted_iota(jnp.int32, shape, 0)
    other = lax.broadcasted_iota(jnp.int32, shape, 1)
    return jnp.where(test(one, other), 1.0, 0.0).astype(BF16)


def lane_mask(rows):
    return lax.broadcasted_iota(jnp.int32, (rows, LANE), 1) < CW


def chunk(x, k):
    low = CW * k
    tile, off = low // LANE, low % LANE
    width = min(2 * LANE, HID - tile * LANE)
    window = x[:, tile * LANE : tile * LANE + width]
    if off:
        window = pltpu.roll(window, width - off, 1)
    return jnp.where(lane_mask(x.shape[0]), window[:, :LANE], 0.0)


def kernel(
    patches_any,
    in_w_any,
    conv_w_any,
    proj_w_any,
    step_w_any,
    step_b_any,
    decay_any,
    skip_any,
    out_w_any,
    out,
    patches,
    in_w,
    conv_w,
    proj_w,
    step_w,
    step_b,
    decay,
    skip,
    out_w,
    halo_send,
    halo_recv,
    pad,
    gate,
    act,
    proj,
    a2a_send,
    raw,
    tokens,
    sw,
    bias,
    rates,
    rates_wide,
    perm,
    tile,
    fold,
    rep,
    step,
    inflow,
    wide_w,
    wide_r,
    ends,
    decays,
    start,
    msg_f32,
    msg,
    cbuf,
    ysum,
    ysend,
    yrecv,
    load_sem,
    halo_ss,
    halo_rs,
    a2a_ss,
    a2a_rs,
    car_ss,
    car_rs,
    ret_ss,
    ret_rs,
):
    R = lax.axis_index("row")
    C = lax.axis_index("col")
    half = lax.rem(C, 2)
    pair = C - half + (1 - half)
    kchunk = lax.div(C, 2)

    barrier = pltpu.get_barrier_semaphore()

    def greet(r, c):
        pl.semaphore_signal(barrier, inc=1, device_id=(r, c), device_id_type=MESH)

    def row_at(o):
        return lax.rem(R + o, ROWS)

    def col_at(o):
        return lax.rem(C + o, COLS)

    for o in range(1, ROWS):
        greet(row_at(o), C)
        greet(row_at(o), pair)
    for o in range(1, COLS):
        greet(R, col_at(o))
    beside = lax.rem(C + 15 + 2 * half, COLS)
    greet(row_at(1), beside)
    greet(row_at(ROWS - 1), beside)

    loads = [
        pltpu.make_async_copy(source, target, load_sem.at[i])
        for i, (source, target) in enumerate(
            (
                (patches_any, patches),
                (in_w_any, in_w),
                (step_w_any, step_w),
                (step_b_any, step_b),
                (decay_any, decay),
                (conv_w_any, conv_w),
                (proj_w_any, proj_w),
                (skip_any, skip),
                (out_w_any, out_w),
            )
        )
    ]
    for copy in loads:
        copy.start()

    picks = zero_one(
        (32, TOK),
        lambda i, t: (t == jnp.where(i < 16, i * TC + TC - 1, (i - 16) * TC))
        & (lax.rem(i, 16) < TR),
    )
    loads[0].wait()
    x = patches[...]
    halo_send[...] = dot(picks, x).astype(BF16)
    pl.semaphore_wait(barrier, 15 + 7 + 7 + 2)

    top, bottom = patches.at[pl.ds(0, 16)], patches.at[pl.ds(TOK - 16, 16)]
    right_edge, left_edge = halo_send.at[pl.ds(0, 16)], halo_send.at[pl.ds(16, 16)]
    rim = (
        (bottom, 1, 0),
        (top, 7, 0),
        (right_edge, 0, 1),
        (left_edge, 0, 15),
        (bottom, 1, 1),
        (bottom, 1, 15),
        (top, 7, 1),
        (top, 7, 15),
    )
    rim_copies = []
    for slot, (edge, dr, dc) in enumerate(rim):
        rim_copies.append(
            pltpu.make_async_remote_copy(
                src_ref=edge,
                dst_ref=halo_recv.at[pl.ds(slot * 16, 16)],
                send_sem=halo_ss.at[slot],
                recv_sem=halo_rs.at[slot],
                device_id=(row_at(dr), col_at(dc)),
                device_id_type=MESH,
            )
        )
    for copy in rim_copies:
        copy.start()

    loads[1].wait()
    normed = normalised(x.astype(F32)).astype(BF16)
    own = dot(normed, in_w[:, :HID]).astype(BF16).astype(F32)
    for i in range(TR):
        pad[1 + i, 8 : 8 + TC, :] = own[i * TC : (i + 1) * TC]
    gate_in = dot(normed, in_w[:, HID:]).astype(BF16).astype(F32)
    gate_silu = silu(gate_in)
    for k in range(KC):
        gate[k] = chunk(gate_silu, k)

    def arrival(p):
        return lax.rem(p, 8) * 32 + lax.rem(lax.div(p, 8), 2) * 16 + lax.div(p, 16)

    perm[0] = zero_one((256, 256), lambda i, j: j == arrival(i))
    perm[1] = zero_one((256, 256), lambda i, j: i == arrival(j))
    tile[...] = zero_one(
        (2 * LANE, QUAD), lambda i, j: lax.rem(i, LANE) == lax.rem(j, CW)
    )
    fold[...] = zero_one((QUAD, LANE), lambda i, j: lax.rem(i, CW) == j)
    for d in range(2):
        for i in range(2):
            first = d * SECOND + RANK + i * NS
            rep[2 * d + i] = zero_one(
                (LANE, STATE), lambda k, j: k - first == lax.div(j, CW)
            )

    for copy in loads[2:5]:
        copy.wait()
    sw[...] = jnp.zeros_like(sw)
    quad_lane = lax.broadcasted_iota(jnp.int32, (NS, QUAD), 1)
    quad_n = lax.broadcasted_iota(jnp.int32, (NS, QUAD), 0)
    own_lanes = lax.div(quad_lane, CW) == lax.rem(quad_n, 4)
    for g in range(2):
        place = kchunk if g == 0 else R
        shift = lax.rem(HID - CW * place, HID)
        for d in range(2):
            branch = g + 2 * d

            def part(value):
                turned = pltpu.roll(value, shift, 1)[:, :LANE]
                return jnp.where(lane_mask(value.shape[0]), turned, 0.0)

            sw[g, d * SECOND : d * SECOND + RANK, d * LANE : (d + 1) * LANE] = part(
                step_w[branch].astype(F32)
            )
            bias[g, :, d * LANE : (d + 1) * LANE] = part(
                jnp.broadcast_to(step_b[branch : branch + 1, :], (8, HID))
            )
            spread = dot(two_parts(part(decay[branch]) * (-LOG2E)), tile[...])
            spread = jnp.where(own_lanes, spread, 0.0)
            b = 2 * g + d
            rates[b] = jnp.zeros((MAP, LANE), F32)
            for m in range(NS // 4):
                four = jnp.sum(spread[4 * m : 4 * m + 4], 0, keepdims=True)
                for kind in range(KIND):
                    j = m * KIND + kind
                    one = four[:, kind * LANE : (kind + 1) * LANE]
                    rates[b, j : j + 1, :] = one
                    rates_wide[b, j * 8 : (j + 1) * 8, :] = jnp.broadcast_to(
                        one, (8, LANE)
                    )
            ends[b, SLOT * SEG :, :] = jnp.zeros(((MAP - SLOT) * SEG, LANE), F32)
            decays[b, SLOT * SEG :, :] = jnp.zeros(((MAP - SLOT) * SEG, LANE), F32)
    place = (R * 2 + half, C)
    for g in range(2):
        cbuf[g, place[g]] = jnp.zeros((MAP, LANE), BF16)

    loads[5].wait()
    loads[6].wait()
    for slot in range(8):
        rim_copies[slot].wait_recv()
    not_first_row = jnp.where(R > 0, 1.0, 0.0)
    not_last_row = jnp.where(R < ROWS - 1, 1.0, 0.0)
    not_first_col = jnp.where(C > 0, 1.0, 0.0)
    not_last_col = jnp.where(C < COLS - 1, 1.0, 0.0)
    rim_in = dot(normalised(halo_recv[...].astype(F32)).astype(BF16), in_w[:, :HID])
    rim_in = rim_in.astype(BF16).astype(F32)
    pad[0, 8 : 8 + TC, :] = rim_in[0:16] * not_first_row
    pad[TR + 1, 8 : 8 + TC, :] = rim_in[16:32] * not_last_row
    left = rim_in[32:48] * not_first_col
    right = rim_in[48:64] * not_last_col
    for i in range(TR):
        pad[1 + i, 7:8, :] = left[i : i + 1]
        pad[1 + i, 8 + TC : 9 + TC, :] = right[i : i + 1]
    pad[0, 7:8, :] = rim_in[79:80] * (not_first_row * not_first_col)
    pad[0, 8 + TC : 9 + TC, :] = rim_in[80:81] * (not_first_row * not_last_col)
    pad[TR + 1, 7:8, :] = rim_in[111:112] * (not_last_row * not_first_col)
    pad[TR + 1, 8 + TC : 9 + TC, :] = rim_in[112:113] * (not_last_row * not_last_col)

    for i in range(TR):
        total = jnp.zeros((TC, HID), F32)
        for p in range(3):
            for q in range(3):
                total = total + pad[i + p, 7 + q : 7 + q + TC, :] * conv_w[p, q : q + 1, :]
        act[i * TC : (i + 1) * TC, :] = silu(total).astype(BF16).astype(F32)

    activated = act[...]
    low = activated.astype(BF16)
    proj[...] = jnp.zeros_like(proj)
    for branch in range(4):
        g, d = branch % 2, branch // 2
        proj[g, :, d * SECOND : d * SECOND + RANK + 2 * NS] = lax.dot_general(
            low, proj_w[branch], (((1,), (1,)), ((), ())), preferred_element_type=F32
        )
    for k in range(KC):
        part_k = chunk(activated, k).astype(BF16)
        for g in range(2):
            a2a_send[g, k, :, :LANE] = part_k
            a2a_send[g, k, :, LANE:] = proj[g].astype(BF16)

    a2a = {0: [], 1: []}
    for o in range(1, ROWS):
        peer = row_at(o)
        a2a[1].append(
            pltpu.make_async_remote_copy(
                src_ref=a2a_send.at[1, peer],
                dst_ref=tokens.at[1, pl.ds(R * TOK, TOK)],
                send_sem=a2a_ss.at[1, o],
                recv_sem=a2a_rs.at[1, o],
                device_id=(peer, C),
                device_id_type=MESH,
            )
        )
    slot = half * 8 + kchunk
    for o in range(1, COLS):
        peer = col_at(o)
        a2a[0].append(
            pltpu.make_async_remote_copy(
                src_ref=a2a_send.at[0, lax.div(peer, 2), pl.ds(lax.rem(peer, 2) * 32, 32)],
                dst_ref=raw.at[pl.ds(slot * 32, 32)],
                send_sem=a2a_ss.at[0, o],
                recv_sem=a2a_rs.at[0, o],
                device_id=(R, peer),
                device_id_type=MESH,
            )
        )
    for g in (1, 0):
        for copy in a2a[g]:
            copy.start()
    tokens[1, pl.ds(R * TOK, TOK), :] = a2a_send[1, R]
    raw[pl.ds(slot * 32, 32), :] = a2a_send[0, kchunk, pl.ds(half * 32, 32), :]

    def peer_of(g, s):
        if g == 0:
            return (lax.div(s, 2), C - half + lax.rem(s, 2))
        return (R, s)

    carries = {0: [], 1: []}
    for g in range(2):
        for o in range(1, PEERS):
            s = lax.rem(place[g] + o, PEERS)
            way = jnp.where(s > place[g], 0, 1)
            carries[g].append(
                pltpu.make_async_remote_copy(
                    src_ref=msg.at[g, way],
                    dst_ref=cbuf.at[g, place[g]],
                    send_sem=car_ss.at[g, o],
                    recv_sem=car_rs.at[g, o],
                    device_id=peer_of(g, s),
                    device_id_type=MESH,
                )
            )

    def scan(b, hf, backward, with_output):
        def body(i, carry):
            held, sums = carry
            pos = POS - 1 - i if backward else i
            row = pl.multiple_of(pos * SEG + hf * 8, 8)
            st = [step[b, pl.ds(row, 8), k * LANE : (k + 1) * LANE] for k in range(KIND)]
            fl = [inflow[b, pl.ds(row, 8), k * LANE : (k + 1) * LANE] for k in range(KIND)]
            new, outs = [], [None] * KIND
            for j in range(SLOT):
                k = j % KIND
                lanes = slice(j * LANE, (j + 1) * LANE)
                a = jnp.exp2(st[k] * rates_wide[b, j * 8 : (j + 1) * 8, :])
                h = a * held[j] + fl[k] * wide_w[b, pl.ds(row, 8), lanes]
                new.append(h)
                if with_output:
                    y = h * wide_r[b, pl.ds(row, 8), lanes]
                    outs[k] = y if outs[k] is None else outs[k] + y
            if with_output:
                for k in range(KIND):
                    ysum[b, pl.ds(row, 8), k * LANE : (k + 1) * LANE] = outs[k]
                return tuple(new), sums
            return tuple(new), tuple(sums[k] + st[k] for k in range(KIND))

        zero = jnp.zeros((8, LANE), F32)
        if with_output:
            first = tuple(
                start[b, j * SEG + hf * 8 : j * SEG + hf * 8 + 8, :] for j in range(SLOT)
            )
            lax.fori_loop(0, POS, body, (first, ()))
            return
        held, sums = lax.fori_loop(
            0, POS, body, ((zero,) * SLOT, (zero,) * KIND)
        )
        for j in range(SLOT):
            at = slice(j * SEG + hf * 8, j * SEG + hf * 8 + 8)
            ends[b, at, :] = held[j]
            decays[b, at, :] = jnp.exp2(
                sums[j % KIND] * rates_wide[b, j * 8 : (j + 1) * 8, :]
            )

    def in_order(d, count):
        return range(count - 1, -1, -1) if d == 1 else range(count)

    def first_pass(g):
        packed = tokens[g, :, LANE:]
        signal = tokens[g, :, :LANE].astype(F32)
        steps = softplus(dot(packed, sw[g].astype(BF16)) + bias[g, 0:1, :])
        for d in range(2):
            b = 2 * g + d
            one = steps[:, d * LANE : (d + 1) * LANE]
            step[b] = dot(two_parts(one), tile[...])
            inflow[b] = dot(two_parts(one * signal), tile[...])
            wide_w[b] = dot(packed, rep[2 * d])
            total = jnp.sum(one, 0, keepdims=True)
            msg_f32[g, d] = jnp.zeros((MAP, LANE), F32)
            for i in range(3):
                piece = total.astype(BF16).astype(F32)
                msg_f32[g, d, SLOT + i : SLOT + i + 1, :] = piece
                total = total - piece
        for d in range(2):
            b = 2 * g + d
            for hf in range(2):
                scan(b, hf, d == 1, False)
            held = jnp.zeros((MAP, LANE), F32)
            for seg in in_order(d, SEG):
                held = (
                    decays[b, pl.ds(seg, MAP, stride=SEG), :] * held
                    + ends[b, pl.ds(seg, MAP, stride=SEG), :]
                )
            msg_f32[g, d, :SLOT, :] = held[:SLOT]
            msg[g, d] = msg_f32[g, d].astype(BF16)
        for copy in carries[g]:
            copy.start()
        for d in range(2):
            wide_r[2 * g + d] = dot(packed, rep[2 * d + 1])

    def second_pass(g):
        maps = cbuf[g].reshape(PEERS * MAP, LANE)
        sums = dot(maps, tile[:LANE, :])
        kind = lax.rem(lax.broadcasted_iota(jnp.int32, (MAP, LANE), 0), KIND)
        factors = []
        for s in range(PEERS):
            at = s * MAP + SLOT
            total = sums[at : at + 1] + sums[at + 1 : at + 2] + sums[at + 2 : at + 3]
            of_slot = jnp.where(
                kind == 0,
                total[:, :LANE],
                jnp.where(kind == 1, total[:, LANE : 2 * LANE], total[:, 2 * LANE :]),
            )
            factors.append(
                jnp.exp2(of_slot * jnp.where(s < place[g], rates[2 * g], rates[2 * g + 1]))
            )
        for d in range(2):
            b = 2 * g + d
            held = jnp.zeros((MAP, LANE), F32)
            for s in in_order(d, PEERS):
                ahead = s > place[g] if d == 1 else s < place[g]
                later = factors[s] * held + cbuf[g, s].astype(F32)
                held = jnp.where(ahead, later, held)
            for seg in in_order(d, SEG):
                start[b, pl.ds(seg, MAP, stride=SEG), :] = held
                held = (
                    decays[b, pl.ds(seg, MAP, stride=SEG), :] * held
                    + ends[b, pl.ds(seg, MAP, stride=SEG), :]
                )
            for hf in range(2):
                scan(b, hf, d == 1, True)
        both = ysum[2 * g] + ysum[2 * g + 1]
        high = both.astype(BF16)
        rest = (both - high.astype(F32)).astype(BF16)
        return (dot(high, fold[...]) + dot(rest, fold[...])).astype(BF16)

    for copy in a2a[1]:
        copy.wait_recv()
    first_pass(1)
    for copy in a2a[0]:
        copy.wait_recv()
    for b in range(2):
        tokens[0, b * 256 : (b + 1) * 256, :] = dot(
            perm[0], raw[b * 256 : (b + 1) * 256, :]
        ).astype(BF16)
    first_pass(0)

    returns = {0: [], 1: []}
    for o in range(1, ROWS):
        peer = row_at(o)
        returns[1].append(
            pltpu.make_async_remote_copy(
                src_ref=ysend.at[1, pl.ds(peer * TOK, TOK)],
                dst_ref=yrecv.at[1, R],
                send_sem=ret_ss.at[1, o],
                recv_sem=ret_rs.at[1, o],
                device_id=(peer, C),
                device_id_type=MESH,
            )
        )
    for o in range(1, COLS):
        peer = col_at(o)
        at = lax.rem(peer, 2) * 8 + lax.div(peer, 2)
        returns[0].append(
            pltpu.make_async_remote_copy(
                src_ref=ysend.at[0, pl.ds(at * 32, 32)],
                dst_ref=yrecv.at[0, kchunk, pl.ds(half * 32, 32)],
                send_sem=ret_ss.at[0, o],
                recv_sem=ret_rs.at[0, o],
                device_id=(R, peer),
                device_id_type=MESH,
            )
        )

    for copy in carries[1]:
        copy.wait_recv()
    ysend[1] = second_pass(1)
    for copy in returns[1]:
        copy.start()
    yrecv[1, R] = ysend[1, pl.ds(R * TOK, TOK), :]

    for copy in carries[0]:
        copy.wait_recv()
    rows_out = second_pass(0)
    for b in range(2):
        ysend[0, b * 256 : (b + 1) * 256, :] = dot(
            perm[1], rows_out[b * 256 : (b + 1) * 256, :]
        ).astype(BF16)
    for copy in returns[0]:
        copy.start()
    yrecv[0, kchunk, pl.ds(half * 32, 32), :] = ysend[0, pl.ds(slot * 32, 32), :]

    loads[7].wait()
    loads[8].wait()
    gains = skip[0:1, :] + skip[1:2, :] + skip[2:3, :] + skip[3:4, :]
    skipped = act[...] * gains
    pieces = [chunk(skipped, k) for k in range(KC)]
    for g in (1, 0):
        for copy in returns[g]:
            copy.wait_recv()
    pieces = [
        pieces[k] + yrecv[0, k].astype(F32) + yrecv[1, k].astype(F32) for k in range(KC)
    ]
    average = sum(jnp.sum(z, -1, keepdims=True) for z in pieces) * (1.0 / HID)
    mask = lane_mask(TOK)
    centred = [jnp.where(mask, z - average, 0.0) for z in pieces]
    variance = sum(jnp.sum(z * z, -1, keepdims=True) for z in centred) * (1.0 / HID)
    scale = lax.rsqrt(variance + epsilon)
    result = jnp.zeros((TOK, CH), F32)
    for k in range(KC):
        gated = (centred[k] * scale * gate[k]).astype(BF16)
        result = result + dot(gated[:, :CW], out_w[k * CW : (k + 1) * CW, :])
    out[...] = result.astype(BF16)

    for copy in rim_copies:
        copy.wait_send()
    for g in range(2):
        for group in (a2a[g], carries[g], returns[g]):
            for copy in group:
                copy.wait_send()


def per_device(
    patches,
    in_weight,
    conv_weight,
    proj_weight,
    step_weight,
    step_bias,
    decay_rate,
    skip_gain,
    out_weight,
):
    vmem = pl.BlockSpec(memory_space=pltpu.VMEM)
    dma = pltpu.SemaphoreType.DMA
    result = pl.pallas_call(
        kernel,
        out_shape=jax.ShapeDtypeStruct((TOK, CH), BF16),
        in_specs=[pl.BlockSpec(memory_space=pl.ANY)] * 9,
        out_specs=vmem,
        scratch_shapes=[
            pltpu.VMEM((TOK, CH), BF16),
            pltpu.VMEM((CH, 2 * HID), BF16),
            pltpu.VMEM((3, 3, HID), F32),
            pltpu.VMEM((4, RANK + 2 * NS, HID), BF16),
            pltpu.VMEM((4, RANK, HID), BF16),
            pltpu.VMEM((4, HID), F32),
            pltpu.VMEM((4, NS, HID), F32),
            pltpu.VMEM((4, HID), F32),
            pltpu.VMEM((HID, CH), BF16),
            pltpu.VMEM((32, CH), BF16),
            pltpu.VMEM((128, CH), BF16),
            pltpu.VMEM((TR + 2, 32, HID), F32),
            pltpu.VMEM((KC, TOK, LANE), F32),
            pltpu.VMEM((TOK, HID), F32),
            pltpu.VMEM((2, TOK, LANE), F32),
            pltpu.VMEM((2, KC, TOK, 2 * LANE), BF16),
            pltpu.VMEM((SPAN, 2 * LANE), BF16),
            pltpu.VMEM((2, SPAN, 2 * LANE), BF16),
            pltpu.VMEM((2, LANE, 2 * LANE), F32),
            pltpu.VMEM((2, 8, 2 * LANE), F32),
            pltpu.VMEM((4, MAP, LANE), F32),
            pltpu.VMEM((4, SLOT * 8, LANE), F32),
            pltpu.VMEM((2, 256, 256), BF16),
            pltpu.VMEM((2 * LANE, QUAD), BF16),
            pltpu.VMEM((QUAD, LANE), BF16),
            pltpu.VMEM((4, LANE, STATE), BF16),
            pltpu.VMEM((4, SPAN, QUAD), F32),
            pltpu.VMEM((4, SPAN, QUAD), F32),
            pltpu.VMEM((4, SPAN, STATE), F32),
            pltpu.VMEM((4, SPAN, STATE), F32),
            pltpu.VMEM((4, MAP * SEG, LANE), F32),
            pltpu.VMEM((4, MAP * SEG, LANE), F32),
            pltpu.VMEM((4, MAP * SEG, LANE), F32),
            pltpu.VMEM((2, 2, MAP, LANE), F32),
            pltpu.VMEM((2, 2, MAP, LANE), BF16),
            pltpu.VMEM((2, PEERS, MAP, LANE), BF16),
            pltpu.VMEM((4, SPAN, QUAD), F32),
            pltpu.VMEM((2, SPAN, LANE), BF16),
            pltpu.VMEM((2, KC, TOK, LANE), BF16),
            dma((9,)),
            dma((8,)),
            dma((8,)),
            dma((2, 16)),
            dma((2, 16)),
            dma((2, 16)),
            dma((2, 16)),
            dma((2, 16)),
            dma((2, 16)),
        ],
        compiler_params=pltpu.CompilerParams(
            collective_id=0, has_side_effects=True, vmem_limit_bytes=63 * 1024 * 1024
        ),
        name="ss2d",
    )(
        patches.reshape(TOK, CH),
        in_weight,
        conv_weight,
        jnp.swapaxes(proj_weight, 1, 2),
        step_weight,
        step_bias,
        decay_rate,
        skip_gain,
        out_weight,
    )
    return result.reshape(TR, TC, CH)


def solution(mesh):
    return jax.shard_map(
        per_device,
        mesh=mesh,
        in_specs=(P("row", "col", None), P(), P(), P(), P(), P(), P(), P(), P()),
        out_specs=P("row", "col", None),
        check_vma=False,
    )
```

```python
import functools

import jax
import jax.numpy as jnp
from jax import lax
from jax.experimental import pallas as pl
from jax.experimental.pallas import tpu as pltpu
from jax.sharding import PartitionSpec as P

MESH = pl.DeviceIdType.MESH
F32, BF16 = jnp.float32, jnp.bfloat16

ROWS, COLS = 8, 16
TR, TC = 4, 16
TOK = TR * TC
RIM = (TR + 2) * TC
CH, HID = 384, 768
RANK, NS = 24, 16
KC = 8
CW = HID // KC
LANE = 128
SECOND = 64
SEG, POS = 16, 32
KIND = 3
QUAD = KIND * LANE
SLOT = NS // 4 * KIND
STATE = SLOT * LANE
MAP = 16
SPAN = SEG * POS
UNROLL = 4
PEERS = 16
LOG2E = 1.4426950408889634
epsilon = 1e-05


def normalised(x):
    average = jnp.mean(x, -1, keepdims=True)
    centred = x - average
    variance = jnp.mean(centred * centred, -1, keepdims=True)
    return centred * lax.rsqrt(variance + epsilon)


def silu(v):
    return v / (1.0 + jnp.exp(-v))


def softplus(v):
    return jnp.maximum(v, 0.0) + jnp.log1p(jnp.exp(-jnp.abs(v)))


def dot(a, b):
    return jnp.dot(a, b, preferred_element_type=F32)


def two_parts(x):
    high = x.astype(BF16)
    return jnp.concatenate([high, (x - high.astype(F32)).astype(BF16)], axis=1)


def zero_one(shape, test):
    one = lax.broadcasted_iota(jnp.int32, shape, 0)
    other = lax.broadcasted_iota(jnp.int32, shape, 1)
    return jnp.where(test(one, other), 1.0, 0.0).astype(BF16)


def lane_mask(rows):
    return lax.broadcasted_iota(jnp.int32, (rows, LANE), 1) < CW


def chunk(x, k):
    low = CW * k
    tile, off = low // LANE, low % LANE
    width = min(2 * LANE, HID - tile * LANE)
    window = x[:, tile * LANE : tile * LANE + width]
    if off:
        window = pltpu.roll(window, width - off, 1)
    return jnp.where(lane_mask(x.shape[0]), window[:, :LANE], 0.0)


def kernel(
    patches_any,
    in_w_any,
    conv_w_any,
    proj_w_any,
    step_w_any,
    step_b_any,
    decay_any,
    skip_any,
    out_w_any,
    out,
    patches,
    in_w,
    conv_w,
    proj_w,
    step_w,
    step_b,
    decay,
    gate_w,
    skip,
    out_w,
    halo_send,
    halo_recv,
    cells,
    shift,
    shifted,
    normed,
    gate,
    act,
    proj,
    a2a_send,
    raw,
    tokens,
    sw,
    bias,
    rates,
    rates_wide,
    perm,
    tile,
    fold,
    rep,
    step,
    inflow,
    wide_w,
    wide_r,
    ends,
    decays,
    start,
    msg_f32,
    msg,
    cbuf,
    ysum,
    ysend,
    yrecv,
    load_sem,
    halo_ss,
    halo_rs,
    a2a_ss,
    a2a_rs,
    car_ss,
    car_rs,
    ret_ss,
    ret_rs,
):
    R = lax.axis_index("row")
    C = lax.axis_index("col")
    half = lax.rem(C, 2)
    pair = C - half + (1 - half)
    kchunk = lax.div(C, 2)

    barrier = pltpu.get_barrier_semaphore()

    def greet(r, c):
        pl.semaphore_signal(barrier, inc=1, device_id=(r, c), device_id_type=MESH)

    def row_at(o):
        return lax.rem(R + o, ROWS)

    def col_at(o):
        return lax.rem(C + o, COLS)

    for o in range(1, ROWS):
        greet(row_at(o), C)
        greet(row_at(o), pair)
    for o in range(1, COLS):
        greet(R, col_at(o))
    beside = lax.rem(C + 15 + 2 * half, COLS)
    greet(row_at(1), beside)
    greet(row_at(ROWS - 1), beside)

    loads = [
        pltpu.make_async_copy(source, target, load_sem.at[i])
        for i, (source, target) in enumerate(
            (
                (patches_any, patches),
                (in_w_any.at[:, pl.ds(0, HID)], in_w),
                (conv_w_any, conv_w),
                (proj_w_any, proj_w),
                (step_w_any, step_w),
                (step_b_any, step_b),
                (decay_any, decay),
                (in_w_any.at[:, pl.ds(HID, HID)], gate_w),
                (skip_any, skip),
                (out_w_any, out_w),
            )
        )
    ]
    for copy in loads:
        copy.start()

    picks = zero_one(
        (32, TOK),
        lambda i, t: (t == jnp.where(i < 16, i * TC + TC - 1, (i - 16) * TC))
        & (lax.rem(i, 16) < TR),
    )
    loads[0].wait()
    x = patches[...]
    halo_send[...] = dot(picks, x).astype(BF16)
    pl.semaphore_wait(barrier, 15 + 7 + 7 + 2)

    top, bottom = patches.at[pl.ds(0, 16)], patches.at[pl.ds(TOK - 16, 16)]
    right_edge, left_edge = halo_send.at[pl.ds(0, 16)], halo_send.at[pl.ds(16, 16)]
    rim = (
        (bottom, 1, 0),
        (top, 7, 0),
        (right_edge, 0, 1),
        (left_edge, 0, 15),
        (bottom, 1, 1),
        (bottom, 1, 15),
        (top, 7, 1),
        (top, 7, 15),
    )
    rim_copies = []
    for slot, (edge, dr, dc) in enumerate(rim):
        rim_copies.append(
            pltpu.make_async_remote_copy(
                src_ref=edge,
                dst_ref=halo_recv.at[pl.ds(slot * 16, 16)],
                send_sem=halo_ss.at[slot],
                recv_sem=halo_rs.at[slot],
                device_id=(row_at(dr), col_at(dc)),
                device_id_type=MESH,
            )
        )
    for copy in rim_copies:
        copy.start()

    loads[1].wait()
    normed[...] = normalised(x.astype(F32)).astype(BF16)
    cells[:TOK, :] = dot(normed[...], in_w[...]).astype(BF16)
    for q in range(3):

        def from_cell(i, j):
            r, c = lax.div(i, TC) - 1, lax.rem(i, TC) + (q - 1)
            above, below, left, right = r < 0, r >= TR, c < 0, c >= TC
            source = jnp.where(above, c, jnp.where(below, TC + c, 0)) + TOK
            source = jnp.where(above | below, source, r * TC + c)
            side = jnp.where(
                above,
                jnp.where(left, 79, 80),
                jnp.where(below, jnp.where(left, 111, 112), jnp.where(left, 32, 48) + r),
            )
            source = jnp.where(left | right, side + TOK, source)
            outside = (above & (R == 0)) | (below & (R == ROWS - 1))
            outside = outside | (left & (C == 0)) | (right & (C == COLS - 1))
            return (j == source) & jnp.logical_not(outside)

        shift[q] = zero_one((RIM, TOK + 128), from_cell)

    for slot in range(8):
        rim_copies[slot].wait_recv()
    cells[TOK:, :] = dot(
        normalised(halo_recv[...].astype(F32)).astype(BF16), in_w[...]
    ).astype(BF16)
    for q in range(3):
        shifted[q] = dot(shift[q], cells[...])
    loads[2].wait()
    for i in range(TR):
        total = jnp.zeros((TC, HID), F32)
        for p in range(3):
            for q in range(3):
                total = total + shifted[q, (i + p) * TC : (i + p + 1) * TC, :] * conv_w[p, q : q + 1, :]
        act[i * TC : (i + 1) * TC, :] = silu(total).astype(BF16).astype(F32)

    activated = act[...]
    low = activated.astype(BF16)
    proj[...] = jnp.zeros_like(proj)
    loads[3].wait()
    for branch in range(4):
        g, d = branch % 2, branch // 2
        proj[g, :, d * SECOND : d * SECOND + RANK + 2 * NS] = lax.dot_general(
            low, proj_w[branch], (((1,), (1,)), ((), ())), preferred_element_type=F32
        )
    for k in range(KC):
        part_k = chunk(activated, k).astype(BF16)
        for g in range(2):
            a2a_send[g, k, :, :LANE] = part_k
            a2a_send[g, k, :, LANE:] = proj[g].astype(BF16)

    a2a = {0: [], 1: []}
    for o in range(1, ROWS):
        peer = row_at(o)
        a2a[1].append(
            pltpu.make_async_remote_copy(
                src_ref=a2a_send.at[1, peer],
                dst_ref=tokens.at[1, pl.ds(R * TOK, TOK)],
                send_sem=a2a_ss.at[1, o],
                recv_sem=a2a_rs.at[1, o],
                device_id=(peer, C),
                device_id_type=MESH,
            )
        )
    slot = half * 8 + kchunk
    for o in range(1, COLS):
        peer = col_at(o)
        a2a[0].append(
            pltpu.make_async_remote_copy(
                src_ref=a2a_send.at[0, lax.div(peer, 2), pl.ds(lax.rem(peer, 2) * 32, 32)],
                dst_ref=raw.at[pl.ds(slot * 32, 32)],
                send_sem=a2a_ss.at[0, o],
                recv_sem=a2a_rs.at[0, o],
                device_id=(R, peer),
                device_id_type=MESH,
            )
        )
    for copy in a2a[1]:
        copy.start()
    tokens[1, pl.ds(R * TOK, TOK), :] = a2a_send[1, R]
    raw[pl.ds(slot * 32, 32), :] = a2a_send[0, kchunk, pl.ds(half * 32, 32), :]

    def arrival(p):
        return lax.rem(p, 8) * 32 + lax.rem(lax.div(p, 8), 2) * 16 + lax.div(p, 16)

    perm[0] = zero_one((256, 256), lambda i, j: j == arrival(i))
    perm[1] = zero_one((256, 256), lambda i, j: i == arrival(j))
    tile[...] = zero_one(
        (2 * LANE, QUAD), lambda i, j: lax.rem(i, LANE) == lax.rem(j, CW)
    )
    fold[...] = zero_one((QUAD, LANE), lambda i, j: lax.rem(i, CW) == j)
    for d in range(2):
        for i in range(2):
            first = d * SECOND + RANK + i * NS
            rep[2 * d + i] = zero_one(
                (LANE, STATE), lambda k, j: k - first == lax.div(j, CW)
            )

    for copy in loads[4:7]:
        copy.wait()
    sw[...] = jnp.zeros_like(sw)
    quad_lane = lax.broadcasted_iota(jnp.int32, (NS, QUAD), 1)
    quad_n = lax.broadcasted_iota(jnp.int32, (NS, QUAD), 0)
    own_lanes = lax.div(quad_lane, CW) == lax.rem(quad_n, 4)
    for g in range(2):
        turn = lax.rem(HID - CW * (kchunk if g == 0 else R), HID)
        for d in range(2):
            branch = g + 2 * d

            def part(value):
                turned = pltpu.roll(value, turn, 1)[:, :LANE]
                return jnp.where(lane_mask(value.shape[0]), turned, 0.0)

            sw[g, d * SECOND : d * SECOND + RANK, d * LANE : (d + 1) * LANE] = part(
                step_w[branch].astype(F32)
            )
            bias[g, :, d * LANE : (d + 1) * LANE] = part(
                jnp.broadcast_to(step_b[branch : branch + 1, :], (8, HID))
            )
            spread = dot(two_parts(part(decay[branch]) * (-LOG2E)), tile[...])
            spread = jnp.where(own_lanes, spread, 0.0)
            b = 2 * g + d
            rates[b] = jnp.zeros((MAP, LANE), F32)
            for m in range(NS // 4):
                four = jnp.sum(spread[4 * m : 4 * m + 4], 0, keepdims=True)
                for kind in range(KIND):
                    j = m * KIND + kind
                    one = four[:, kind * LANE : (kind + 1) * LANE]
                    rates[b, j : j + 1, :] = one
                    rates_wide[b, j * 8 : (j + 1) * 8, :] = jnp.broadcast_to(
                        one, (8, LANE)
                    )
            ends[b, SLOT * SEG :, :] = jnp.zeros(((MAP - SLOT) * SEG, LANE), F32)
            decays[b, SLOT * SEG :, :] = jnp.zeros(((MAP - SLOT) * SEG, LANE), F32)
    place = (R * 2 + half, C)
    for g in range(2):
        cbuf[g, place[g]] = jnp.zeros((MAP, LANE), BF16)

    for copy in a2a[0]:
        copy.start()

    def peer_of(g, s):
        if g == 0:
            return (lax.div(s, 2), C - half + lax.rem(s, 2))
        return (R, s)

    carries = {0: [], 1: []}
    for g in range(2):
        for o in range(1, PEERS):
            s = lax.rem(place[g] + o, PEERS)
            way = jnp.where(s > place[g], 0, 1)
            carries[g].append(
                pltpu.make_async_remote_copy(
                    src_ref=msg.at[g, way],
                    dst_ref=cbuf.at[g, place[g]],
                    send_sem=car_ss.at[g, o],
                    recv_sem=car_rs.at[g, o],
                    device_id=peer_of(g, s),
                    device_id_type=MESH,
                )
            )

    def scan(b, hf, backward, with_output):
        rate = [rates_wide[b, j * 8 : (j + 1) * 8, :] for j in range(SLOT)]

        def body(i, carry):
            held, sums = carry
            pos = POS - 1 - i if backward else i
            row = pl.multiple_of(pos * SEG + hf * 8, 8)
            st = [step[b, pl.ds(row, 8), k * LANE : (k + 1) * LANE] for k in range(KIND)]
            fl = [inflow[b, pl.ds(row, 8), k * LANE : (k + 1) * LANE] for k in range(KIND)]
            new, outs = [], [None] * KIND
            for j in range(SLOT):
                k = j % KIND
                lanes = slice(j * LANE, (j + 1) * LANE)
                a = jnp.exp2(st[k] * rate[j])
                h = a * held[j] + fl[k] * wide_w[b, pl.ds(row, 8), lanes]
                new.append(h)
                if with_output:
                    y = h * wide_r[b, pl.ds(row, 8), lanes]
                    outs[k] = y if outs[k] is None else outs[k] + y
            if with_output:
                for k in range(KIND):
                    ysum[b, pl.ds(row, 8), k * LANE : (k + 1) * LANE] = outs[k]
                return tuple(new), sums
            return tuple(new), tuple(sums[k] + st[k] for k in range(KIND))

        zero = jnp.zeros((8, LANE), F32)
        if with_output:
            first = tuple(
                start[b, j * SEG + hf * 8 : j * SEG + hf * 8 + 8, :] for j in range(SLOT)
            )
            lax.fori_loop(0, POS, body, (first, ()), unroll=UNROLL)
            return
        held, sums = lax.fori_loop(
            0, POS, body, ((zero,) * SLOT, (zero,) * KIND), unroll=UNROLL
        )
        for j in range(SLOT):
            at = slice(j * SEG + hf * 8, j * SEG + hf * 8 + 8)
            ends[b, at, :] = held[j]
            decays[b, at, :] = jnp.exp2(
                sums[j % KIND] * rates_wide[b, j * 8 : (j + 1) * 8, :]
            )

    def in_order(d, count):
        return range(count - 1, -1, -1) if d == 1 else range(count)

    def first_pass(g):
        packed = tokens[g, :, LANE:]
        signal = tokens[g, :, :LANE].astype(F32)
        steps = softplus(dot(packed, sw[g].astype(BF16)) + bias[g, 0:1, :])
        for d in range(2):
            b = 2 * g + d
            one = steps[:, d * LANE : (d + 1) * LANE]
            step[b] = dot(two_parts(one), tile[...])
            inflow[b] = dot(two_parts(one * signal), tile[...])
            wide_w[b] = dot(packed, rep[2 * d])
            total = jnp.sum(one, 0, keepdims=True)
            msg_f32[g, d] = jnp.zeros((MAP, LANE), F32)
            for i in range(3):
                piece = total.astype(BF16).astype(F32)
                msg_f32[g, d, SLOT + i : SLOT + i + 1, :] = piece
                total = total - piece
        for d in range(2):
            b = 2 * g + d
            for hf in range(2):
                scan(b, hf, d == 1, False)
            held = jnp.zeros((MAP, LANE), F32)
            for seg in in_order(d, SEG):
                held = (
                    decays[b, pl.ds(seg, MAP, stride=SEG), :] * held
                    + ends[b, pl.ds(seg, MAP, stride=SEG), :]
                )
            msg_f32[g, d, :SLOT, :] = held[:SLOT]
            msg[g, d] = msg_f32[g, d].astype(BF16)
        for copy in carries[g]:
            copy.start()

    def second_pass(g):
        maps = cbuf[g].reshape(PEERS * MAP, LANE)
        sums = dot(maps, tile[:LANE, :])
        kind = lax.rem(lax.broadcasted_iota(jnp.int32, (MAP, LANE), 0), KIND)
        factors = []
        for s in range(PEERS):
            at = s * MAP + SLOT
            total = sums[at : at + 1] + sums[at + 1 : at + 2] + sums[at + 2 : at + 3]
            of_slot = jnp.where(
                kind == 0,
                total[:, :LANE],
                jnp.where(kind == 1, total[:, LANE : 2 * LANE], total[:, 2 * LANE :]),
            )
            factors.append(
                jnp.exp2(of_slot * jnp.where(s < place[g], rates[2 * g], rates[2 * g + 1]))
            )
        for d in range(2):
            b = 2 * g + d
            held = jnp.zeros((MAP, LANE), F32)
            for s in in_order(d, PEERS):
                ahead = s > place[g] if d == 1 else s < place[g]
                later = factors[s] * held + cbuf[g, s].astype(F32)
                held = jnp.where(ahead, later, held)
            for seg in in_order(d, SEG):
                start[b, pl.ds(seg, MAP, stride=SEG), :] = held
                held = (
                    decays[b, pl.ds(seg, MAP, stride=SEG), :] * held
                    + ends[b, pl.ds(seg, MAP, stride=SEG), :]
                )
            for hf in range(2):
                scan(b, hf, d == 1, True)
        both = ysum[2 * g] + ysum[2 * g + 1]
        high = both.astype(BF16)
        rest = (both - high.astype(F32)).astype(BF16)
        return (dot(high, fold[...]) + dot(rest, fold[...])).astype(BF16)

    for copy in a2a[1]:
        copy.wait_recv()
    first_pass(1)
    for copy in a2a[0]:
        copy.wait_recv()
    for b in range(2):
        tokens[0, b * 256 : (b + 1) * 256, :] = dot(
            perm[0], raw[b * 256 : (b + 1) * 256, :]
        ).astype(BF16)
    first_pass(0)
    for g in (1, 0):
        for d in range(2):
            wide_r[2 * g + d] = dot(tokens[g, :, LANE:], rep[2 * d + 1])

    returns = {0: [], 1: []}
    for o in range(1, ROWS):
        peer = row_at(o)
        returns[1].append(
            pltpu.make_async_remote_copy(
                src_ref=ysend.at[1, pl.ds(peer * TOK, TOK)],
                dst_ref=yrecv.at[1, R],
                send_sem=ret_ss.at[1, o],
                recv_sem=ret_rs.at[1, o],
                device_id=(peer, C),
                device_id_type=MESH,
            )
        )
    for o in range(1, COLS):
        peer = col_at(o)
        at = lax.rem(peer, 2) * 8 + lax.div(peer, 2)
        returns[0].append(
            pltpu.make_async_remote_copy(
                src_ref=ysend.at[0, pl.ds(at * 32, 32)],
                dst_ref=yrecv.at[0, kchunk, pl.ds(half * 32, 32)],
                send_sem=ret_ss.at[0, o],
                recv_sem=ret_rs.at[0, o],
                device_id=(R, peer),
                device_id_type=MESH,
            )
        )

    for copy in carries[1]:
        copy.wait_recv()
    ysend[1] = second_pass(1)
    for copy in returns[1]:
        copy.start()
    yrecv[1, R] = ysend[1, pl.ds(R * TOK, TOK), :]

    for copy in carries[0]:
        copy.wait_recv()
    rows_out = second_pass(0)
    for b in range(2):
        ysend[0, b * 256 : (b + 1) * 256, :] = dot(
            perm[1], rows_out[b * 256 : (b + 1) * 256, :]
        ).astype(BF16)
    for copy in returns[0]:
        copy.start()
    yrecv[0, kchunk, pl.ds(half * 32, 32), :] = ysend[0, pl.ds(slot * 32, 32), :]

    for copy in loads[7:]:
        copy.wait()
    gate_in = dot(normed[...], gate_w[...]).astype(BF16).astype(F32)
    gate_silu = silu(gate_in)
    for k in range(KC):
        gate[k] = chunk(gate_silu, k)
    gains = skip[0:1, :] + skip[1:2, :] + skip[2:3, :] + skip[3:4, :]
    skipped = act[...] * gains
    pieces = [chunk(skipped, k) for k in range(KC)]
    for g in (1, 0):
        for copy in returns[g]:
            copy.wait_recv()
    pieces = [
        pieces[k] + yrecv[0, k].astype(F32) + yrecv[1, k].astype(F32) for k in range(KC)
    ]
    average = jnp.sum(sum(pieces), -1, keepdims=True) * (1.0 / HID)
    mask = lane_mask(TOK)
    centred = [jnp.where(mask, z - average, 0.0) for z in pieces]
    variance = jnp.sum(sum(z * z for z in centred), -1, keepdims=True) * (1.0 / HID)
    scale = lax.rsqrt(variance + epsilon)
    result = jnp.zeros((TOK, CH), F32)
    for k in range(KC):
        gated = (centred[k] * scale * gate[k]).astype(BF16)
        result = result + dot(gated[:, :CW], out_w[k * CW : (k + 1) * CW, :])
    out[...] = result.astype(BF16)

    for copy in rim_copies:
        copy.wait_send()
    for g in range(2):
        for group in (a2a[g], carries[g], returns[g]):
            for copy in group:
                copy.wait_send()


def per_device(
    patches,
    in_weight,
    conv_weight,
    proj_weight,
    step_weight,
    step_bias,
    decay_rate,
    skip_gain,
    out_weight,
):
    vmem = pl.BlockSpec(memory_space=pltpu.VMEM)
    dma = pltpu.SemaphoreType.DMA
    result = pl.pallas_call(
        kernel,
        out_shape=jax.ShapeDtypeStruct((TOK, CH), BF16),
        in_specs=[pl.BlockSpec(memory_space=pl.ANY)] * 9,
        out_specs=vmem,
        scratch_shapes=[
            pltpu.VMEM((TOK, CH), BF16),
            pltpu.VMEM((CH, HID), BF16),
            pltpu.VMEM((3, 3, HID), F32),
            pltpu.VMEM((4, RANK + 2 * NS, HID), BF16),
            pltpu.VMEM((4, RANK, HID), BF16),
            pltpu.VMEM((4, HID), F32),
            pltpu.VMEM((4, NS, HID), F32),
            pltpu.VMEM((CH, HID), BF16),
            pltpu.VMEM((4, HID), F32),
            pltpu.VMEM((HID, CH), BF16),
            pltpu.VMEM((32, CH), BF16),
            pltpu.VMEM((128, CH), BF16),
            pltpu.VMEM((TOK + 128, HID), BF16),
            pltpu.VMEM((3, RIM, TOK + 128), BF16),
            pltpu.VMEM((3, RIM, HID), F32),
            pltpu.VMEM((TOK, CH), BF16),
            pltpu.VMEM((KC, TOK, LANE), F32),
            pltpu.VMEM((TOK, HID), F32),
            pltpu.VMEM((2, TOK, LANE), F32),
            pltpu.VMEM((2, KC, TOK, 2 * LANE), BF16),
            pltpu.VMEM((SPAN, 2 * LANE), BF16),
            pltpu.VMEM((2, SPAN, 2 * LANE), BF16),
            pltpu.VMEM((2, LANE, 2 * LANE), F32),
            pltpu.VMEM((2, 8, 2 * LANE), F32),
            pltpu.VMEM((4, MAP, LANE), F32),
            pltpu.VMEM((4, SLOT * 8, LANE), F32),
            pltpu.VMEM((2, 256, 256), BF16),
            pltpu.VMEM((2 * LANE, QUAD), BF16),
            pltpu.VMEM((QUAD, LANE), BF16),
            pltpu.VMEM((4, LANE, STATE), BF16),
            pltpu.VMEM((4, SPAN, QUAD), F32),
            pltpu.VMEM((4, SPAN, QUAD), F32),
            pltpu.VMEM((4, SPAN, STATE), F32),
            pltpu.VMEM((4, SPAN, STATE), F32),
            pltpu.VMEM((4, MAP * SEG, LANE), F32),
            pltpu.VMEM((4, MAP * SEG, LANE), F32),
            pltpu.VMEM((4, MAP * SEG, LANE), F32),
            pltpu.VMEM((2, 2, MAP, LANE), F32),
            pltpu.VMEM((2, 2, MAP, LANE), BF16),
            pltpu.VMEM((2, PEERS, MAP, LANE), BF16),
            pltpu.VMEM((4, SPAN, QUAD), F32),
            pltpu.VMEM((2, SPAN, LANE), BF16),
            pltpu.VMEM((2, KC, TOK, LANE), BF16),
            dma((10,)),
            dma((8,)),
            dma((8,)),
            dma((2, 16)),
            dma((2, 16)),
            dma((2, 16)),
            dma((2, 16)),
            dma((2, 16)),
            dma((2, 16)),
        ],
        compiler_params=pltpu.CompilerParams(
            collective_id=0, has_side_effects=True, vmem_limit_bytes=63 * 1024 * 1024
        ),
        name="ss2d",
    )(
        patches.reshape(TOK, CH),
        in_weight,
        conv_weight,
        jnp.swapaxes(proj_weight, 1, 2),
        step_weight,
        step_bias,
        decay_rate,
        skip_gain,
        out_weight,
    )
    return result.reshape(TR, TC, CH)


def solution(mesh):
    return jax.shard_map(
        per_device,
        mesh=mesh,
        in_specs=(P("row", "col", None), P(), P(), P(), P(), P(), P(), P(), P()),
        out_specs=P("row", "col", None),
        check_vma=False,
    )
```

```python
import functools

import jax
import jax.numpy as jnp
from jax import lax
from jax.experimental import pallas as pl
from jax.experimental.pallas import tpu as pltpu
from jax.sharding import PartitionSpec as P

MESH = pl.DeviceIdType.MESH
F32, BF16 = jnp.float32, jnp.bfloat16

ROWS, COLS = 8, 16
TR, TC = 4, 16
TOK = TR * TC
RIM = (TR + 2) * TC
CH, HID = 384, 768
RANK, NS = 24, 16
KC = 8
CW = HID // KC
LANE = 128
SECOND = 64
SEG, POS = 16, 32
GROUP = 16
KIND = CW // GROUP
WIDE = KIND * LANE
SLOT = 2 * KIND
BOTH = 2 * LANE
MAP = 16
SPAN = SEG * POS
TURN = 4
PEERS = 16
LOG2E = 1.4426950408889634
epsilon = 1e-05


def normalised(x):
    average = jnp.mean(x, -1, keepdims=True)
    centred = x - average
    variance = jnp.mean(centred * centred, -1, keepdims=True)
    return centred * lax.rsqrt(variance + epsilon)


def silu(v):
    return v / (1.0 + jnp.exp(-v))


def softplus(v):
    return jnp.maximum(v, 0.0) + jnp.log1p(jnp.exp(-jnp.abs(v)))


def dot(a, b):
    return jnp.dot(a, b, preferred_element_type=F32)


def two_parts(x):
    high = x.astype(BF16)
    return jnp.concatenate([high, (x - high.astype(F32)).astype(BF16)], axis=1)


def zero_one(shape, test):
    one = lax.broadcasted_iota(jnp.int32, shape, 0)
    other = lax.broadcasted_iota(jnp.int32, shape, 1)
    return jnp.where(test(one, other), 1.0, 0.0).astype(BF16)


def lane_mask(rows):
    return lax.broadcasted_iota(jnp.int32, (rows, LANE), 1) < CW


def chunk(x, k):
    low = CW * k
    tile, off = low // LANE, low % LANE
    width = min(2 * LANE, HID - tile * LANE)
    window = x[:, tile * LANE : tile * LANE + width]
    if off:
        window = pltpu.roll(window, width - off, 1)
    return jnp.where(lane_mask(x.shape[0]), window[:, :LANE], 0.0)


def kernel(
    patches_any,
    in_w_any,
    conv_w_any,
    proj_w_any,
    step_w_any,
    step_b_any,
    decay_any,
    skip_any,
    out_w_any,
    out,
    patches,
    in_w,
    conv_w,
    proj_w,
    step_w,
    step_b,
    decay,
    gate_w,
    skip,
    out_w,
    halo_send,
    halo_recv,
    cells,
    shift,
    shifted,
    normed,
    gate,
    act,
    proj,
    a2a_send,
    raw,
    tokens,
    sw,
    bias,
    rates,
    rates_wide,
    perm,
    tile,
    fold,
    gather,
    rep,
    step,
    inflow,
    wide,
    ends,
    decays,
    start,
    msg_f32,
    msg,
    cbuf,
    ysum,
    ysend,
    yrecv,
    load_sem,
    halo_ss,
    halo_rs,
    a2a_ss,
    a2a_rs,
    car_ss,
    car_rs,
    ret_ss,
    ret_rs,
):
    R = lax.axis_index("row")
    C = lax.axis_index("col")
    half = lax.rem(C, 2)
    pair = C - half + (1 - half)
    kchunk = lax.div(C, 2)

    barrier = pltpu.get_barrier_semaphore()

    def greet(r, c):
        pl.semaphore_signal(barrier, inc=1, device_id=(r, c), device_id_type=MESH)

    def row_at(o):
        return lax.rem(R + o, ROWS)

    def col_at(o):
        return lax.rem(C + o, COLS)

    for o in range(1, ROWS):
        greet(row_at(o), C)
        greet(row_at(o), pair)
    for o in range(1, COLS):
        greet(R, col_at(o))
    beside = lax.rem(C + 15 + 2 * half, COLS)
    greet(row_at(1), beside)
    greet(row_at(ROWS - 1), beside)

    loads = [
        pltpu.make_async_copy(source, target, load_sem.at[i])
        for i, (source, target) in enumerate(
            (
                (patches_any, patches),
                (in_w_any.at[:, pl.ds(0, HID)], in_w),
                (conv_w_any, conv_w),
                (proj_w_any, proj_w),
                (step_w_any, step_w),
                (step_b_any, step_b),
                (decay_any, decay),
                (in_w_any.at[:, pl.ds(HID, HID)], gate_w),
                (skip_any, skip),
                (out_w_any, out_w),
            )
        )
    ]
    for copy in loads:
        copy.start()

    picks = zero_one(
        (32, TOK),
        lambda i, t: (t == jnp.where(i < 16, i * TC + TC - 1, (i - 16) * TC))
        & (lax.rem(i, 16) < TR),
    )
    loads[0].wait()
    x = patches[...]
    halo_send[...] = dot(picks, x).astype(BF16)
    pl.semaphore_wait(barrier, 15 + 7 + 7 + 2)

    top, bottom = patches.at[pl.ds(0, 16)], patches.at[pl.ds(TOK - 16, 16)]
    right_edge, left_edge = halo_send.at[pl.ds(0, 16)], halo_send.at[pl.ds(16, 16)]
    rim = (
        (bottom, 1, 0),
        (top, 7, 0),
        (right_edge, 0, 1),
        (left_edge, 0, 15),
        (bottom, 1, 1),
        (bottom, 1, 15),
        (top, 7, 1),
        (top, 7, 15),
    )
    rim_copies = []
    for slot, (edge, dr, dc) in enumerate(rim):
        rim_copies.append(
            pltpu.make_async_remote_copy(
                src_ref=edge,
                dst_ref=halo_recv.at[pl.ds(slot * 16, 16)],
                send_sem=halo_ss.at[slot],
                recv_sem=halo_rs.at[slot],
                device_id=(row_at(dr), col_at(dc)),
                device_id_type=MESH,
            )
        )
    for copy in rim_copies:
        copy.start()

    loads[1].wait()
    normed[...] = normalised(x.astype(F32)).astype(BF16)
    cells[:TOK, :] = dot(normed[...], in_w[...]).astype(BF16)
    for q in range(3):

        def from_cell(i, j):
            r, c = lax.div(i, TC) - 1, lax.rem(i, TC) + (q - 1)
            above, below, left, right = r < 0, r >= TR, c < 0, c >= TC
            source = jnp.where(above, c, jnp.where(below, TC + c, 0)) + TOK
            source = jnp.where(above | below, source, r * TC + c)
            side = jnp.where(
                above,
                jnp.where(left, 79, 80),
                jnp.where(below, jnp.where(left, 111, 112), jnp.where(left, 32, 48) + r),
            )
            source = jnp.where(left | right, side + TOK, source)
            outside = (above & (R == 0)) | (below & (R == ROWS - 1))
            outside = outside | (left & (C == 0)) | (right & (C == COLS - 1))
            return (j == source) & jnp.logical_not(outside)

        shift[q] = zero_one((RIM, TOK + 128), from_cell)

    for slot in range(8):
        rim_copies[slot].wait_recv()
    cells[TOK:, :] = dot(
        normalised(halo_recv[...].astype(F32)).astype(BF16), in_w[...]
    ).astype(BF16)
    for q in range(3):
        shifted[q] = dot(shift[q], cells[...])
    loads[2].wait()
    for i in range(TR):
        total = jnp.zeros((TC, HID), F32)
        for p in range(3):
            for q in range(3):
                total = total + shifted[q, (i + p) * TC : (i + p + 1) * TC, :] * conv_w[p, q : q + 1, :]
        act[i * TC : (i + 1) * TC, :] = silu(total).astype(BF16).astype(F32)

    activated = act[...]
    low = activated.astype(BF16)
    proj[...] = jnp.zeros_like(proj)
    loads[3].wait()
    for branch in range(4):
        g, d = branch % 2, branch // 2
        proj[g, :, d * SECOND : d * SECOND + RANK + 2 * NS] = lax.dot_general(
            low, proj_w[branch], (((1,), (1,)), ((), ())), preferred_element_type=F32
        )
    for k in range(KC):
        part_k = chunk(activated, k).astype(BF16)
        for g in range(2):
            a2a_send[g, k, :, :LANE] = part_k
            a2a_send[g, k, :, LANE:] = proj[g].astype(BF16)

    a2a = {0: [], 1: []}
    for o in range(1, ROWS):
        peer = row_at(o)
        a2a[1].append(
            pltpu.make_async_remote_copy(
                src_ref=a2a_send.at[1, peer],
                dst_ref=tokens.at[1, pl.ds(R * TOK, TOK)],
                send_sem=a2a_ss.at[1, o],
                recv_sem=a2a_rs.at[1, o],
                device_id=(peer, C),
                device_id_type=MESH,
            )
        )
    slot = half * 8 + kchunk
    for o in range(1, COLS):
        peer = col_at(o)
        a2a[0].append(
            pltpu.make_async_remote_copy(
                src_ref=a2a_send.at[0, lax.div(peer, 2), pl.ds(lax.rem(peer, 2) * 32, 32)],
                dst_ref=raw.at[pl.ds(slot * 32, 32)],
                send_sem=a2a_ss.at[0, o],
                recv_sem=a2a_rs.at[0, o],
                device_id=(R, peer),
                device_id_type=MESH,
            )
        )
    for copy in a2a[1]:
        copy.start()
    tokens[1, pl.ds(R * TOK, TOK), :] = a2a_send[1, R]
    raw[pl.ds(slot * 32, 32), :] = a2a_send[0, kchunk, pl.ds(half * 32, 32), :]

    def arrival(p):
        return lax.rem(p, 8) * 32 + lax.rem(lax.div(p, 8), 2) * 16 + lax.div(p, 16)

    perm[0] = zero_one((256, 256), lambda i, j: j == arrival(i))
    perm[1] = zero_one((256, 256), lambda i, j: i == arrival(j))

    def channel(j):
        return lax.div(j, LANE) * GROUP + lax.rem(j, GROUP)

    tile[...] = zero_one((2 * LANE, WIDE), lambda i, j: lax.rem(i, LANE) == channel(j))
    fold[...] = zero_one((WIDE, LANE), lambda i, j: channel(i) == j)
    gather[...] = zero_one((SEG, SPAN), lambda i, j: i == lax.rem(j, SEG))
    for d in range(2):
        for i in range(2):
            first = d * SECOND + RANK + i * NS
            at = (2 * d + i) * BOTH
            rep[:, at : at + BOTH] = zero_one(
                (LANE, BOTH), lambda k, j: k - first == lax.div(j, GROUP)
            )

    for copy in loads[4:7]:
        copy.wait()
    sw[...] = jnp.zeros_like(sw)
    wide_lane = lax.broadcasted_iota(jnp.int32, (NS, WIDE), 1)
    wide_n = lax.broadcasted_iota(jnp.int32, (NS, WIDE), 0)
    own_lanes = lax.div(lax.rem(wide_lane, LANE), GROUP) == lax.rem(wide_n, 8)
    for g in range(2):
        turn = lax.rem(HID - CW * (kchunk if g == 0 else R), HID)
        for d in range(2):
            branch = g + 2 * d

            def part(value):
                turned = pltpu.roll(value, turn, 1)[:, :LANE]
                return jnp.where(lane_mask(value.shape[0]), turned, 0.0)

            sw[g, d * SECOND : d * SECOND + RANK, d * LANE : (d + 1) * LANE] = part(
                step_w[branch].astype(F32)
            )
            bias[g, :, d * LANE : (d + 1) * LANE] = part(
                jnp.broadcast_to(step_b[branch : branch + 1, :], (8, HID))
            )
            spread = dot(two_parts(part(decay[branch]) * (-LOG2E)), tile[...])
            spread = jnp.where(own_lanes, spread, 0.0)
            b = 2 * g + d
            rates[b] = jnp.zeros((MAP, LANE), F32)
            for m in range(2):
                eight = jnp.sum(spread[8 * m : 8 * m + 8], 0, keepdims=True)
                for kind in range(KIND):
                    j = m * KIND + kind
                    one = eight[:, kind * LANE : (kind + 1) * LANE]
                    rates[b, j : j + 1, :] = one
                    rates_wide[b, j * 8 : (j + 1) * 8, :] = jnp.broadcast_to(
                        one, (8, LANE)
                    )
            ends[b, SLOT * SEG :, :] = jnp.zeros(((MAP - SLOT) * SEG, LANE), F32)
            decays[b, SLOT * SEG :, :] = jnp.zeros(((MAP - SLOT) * SEG, LANE), F32)
    place = (R * 2 + half, C)
    for g in range(2):
        cbuf[g, place[g]] = jnp.zeros((MAP, LANE), BF16)

    for copy in a2a[0]:
        copy.start()

    def peer_of(g, s):
        if g == 0:
            return (lax.div(s, 2), C - half + lax.rem(s, 2))
        return (R, s)

    carries = {0: [], 1: []}
    for g in range(2):
        for o in range(1, PEERS):
            s = lax.rem(place[g] + o, PEERS)
            way = jnp.where(s > place[g], 0, 1)
            carries[g].append(
                pltpu.make_async_remote_copy(
                    src_ref=msg.at[g, way],
                    dst_ref=cbuf.at[g, place[g]],
                    send_sem=car_ss.at[g, o],
                    recv_sem=car_rs.at[g, o],
                    device_id=peer_of(g, s),
                    device_id_type=MESH,
                )
            )

    def scan(b, hf, backward, with_output):
        g, d = b // 2, b % 2
        rate = [rates_wide[b, j * 8 : (j + 1) * 8, :] for j in range(SLOT)]

        def body(i, held):
            for u in range(TURN):
                pos = i * TURN + u
                pos = POS - 1 - pos if backward else pos
                rows = pl.ds(pl.multiple_of(pos * SEG + hf * 8, 8), 8)

                def part(ref, at, k):
                    return ref[at, rows, k * LANE : (k + 1) * LANE]

                st = [part(step, b, k) for k in range(KIND)]
                fl = [part(inflow, b, k) for k in range(KIND)]
                w = [part(wide, g, 4 * d + m) for m in range(2)]
                r = [part(wide, g, 4 * d + 2 + m) for m in range(2)] if with_output else None
                new, outs = [], [None] * KIND
                for j in range(SLOT):
                    m, k = j // KIND, j % KIND
                    h = jnp.exp2(st[k] * rate[j]) * held[j] + fl[k] * w[m]
                    new.append(h)
                    if with_output:
                        y = h * r[m]
                        outs[k] = y if outs[k] is None else outs[k] + y
                held = tuple(new)
                if with_output:
                    for k in range(KIND):
                        y = outs[k] + part(ysum, g, k) if d == 1 else outs[k]
                        ysum[g, rows, k * LANE : (k + 1) * LANE] = y
            return held

        if with_output:
            first = tuple(
                start[b, j * SEG + hf * 8 : j * SEG + hf * 8 + 8, :] for j in range(SLOT)
            )
            lax.fori_loop(0, POS // TURN, body, first)
            return
        zero = jnp.zeros((8, LANE), F32)
        held = lax.fori_loop(0, POS // TURN, body, (zero,) * SLOT)
        for j in range(SLOT):
            ends[b, j * SEG + hf * 8 : j * SEG + hf * 8 + 8, :] = held[j]

    def in_order(d, count):
        return range(count - 1, -1, -1) if d == 1 else range(count)

    def first_pass(g):
        packed = tokens[g, :, LANE:]
        signal = dot(tokens[g, :, :LANE], tile[:LANE, :])
        steps = softplus(dot(packed, sw[g].astype(BF16)) + bias[g, 0:1, :])
        wide[g] = dot(packed, rep[...])
        for d in range(2):
            b = 2 * g + d
            parts = two_parts(steps[:, d * LANE : (d + 1) * LANE])
            step[b] = dot(parts, tile[...])
            inflow[b] = step[b] * signal
            sums = dot(gather[...], parts)
            sums = sums[:, :LANE] + sums[:, LANE:]
            of_lanes = dot(two_parts(sums), tile[...])
            for j in range(SLOT):
                k = j % KIND
                decays[b, j * SEG : (j + 1) * SEG, :] = jnp.exp2(
                    of_lanes[:, k * LANE : (k + 1) * LANE] * rates[b, j : j + 1, :]
                )
            total = jnp.sum(sums, 0, keepdims=True)
            msg_f32[g, d] = jnp.zeros((MAP, LANE), F32)
            for i in range(3):
                piece = total.astype(BF16).astype(F32)
                msg_f32[g, d, SLOT + i : SLOT + i + 1, :] = piece
                total = total - piece
        for d in range(2):
            b = 2 * g + d
            for hf in range(2):
                scan(b, hf, d == 1, False)
            held = jnp.zeros((MAP, LANE), F32)
            for seg in in_order(d, SEG):
                held = (
                    decays[b, pl.ds(seg, MAP, stride=SEG), :] * held
                    + ends[b, pl.ds(seg, MAP, stride=SEG), :]
                )
            msg_f32[g, d, :SLOT, :] = held[:SLOT]
            msg[g, d] = msg_f32[g, d].astype(BF16)
        for copy in carries[g]:
            copy.start()

    def second_pass(g):
        maps = cbuf[g].reshape(PEERS * MAP, LANE)
        sums = dot(maps, tile[:LANE, :])
        kind = lax.rem(lax.broadcasted_iota(jnp.int32, (MAP, LANE), 0), KIND)
        factors = []
        for s in range(PEERS):
            at = s * MAP + SLOT
            total = sums[at : at + 1] + sums[at + 1 : at + 2] + sums[at + 2 : at + 3]
            of_slot = total[:, :LANE]
            for k in range(1, KIND):
                of_slot = jnp.where(kind == k, total[:, k * LANE : (k + 1) * LANE], of_slot)
            factors.append(
                jnp.exp2(of_slot * jnp.where(s < place[g], rates[2 * g], rates[2 * g + 1]))
            )
        for d in range(2):
            b = 2 * g + d
            held = jnp.zeros((MAP, LANE), F32)
            for s in in_order(d, PEERS):
                ahead = s > place[g] if d == 1 else s < place[g]
                later = factors[s] * held + cbuf[g, s].astype(F32)
                held = jnp.where(ahead, later, held)
            for seg in in_order(d, SEG):
                start[b, pl.ds(seg, MAP, stride=SEG), :] = held
                held = (
                    decays[b, pl.ds(seg, MAP, stride=SEG), :] * held
                    + ends[b, pl.ds(seg, MAP, stride=SEG), :]
                )
            for hf in range(2):
                scan(b, hf, d == 1, True)
        return dot(ysum[g].astype(BF16), fold[...]).astype(BF16)

    for copy in a2a[1]:
        copy.wait_recv()
    first_pass(1)
    for copy in a2a[0]:
        copy.wait_recv()
    for b in range(2):
        tokens[0, b * 256 : (b + 1) * 256, :] = dot(
            perm[0], raw[b * 256 : (b + 1) * 256, :]
        ).astype(BF16)
    first_pass(0)
    returns = {0: [], 1: []}
    for o in range(1, ROWS):
        peer = row_at(o)
        returns[1].append(
            pltpu.make_async_remote_copy(
                src_ref=ysend.at[1, pl.ds(peer * TOK, TOK)],
                dst_ref=yrecv.at[1, R],
                send_sem=ret_ss.at[1, o],
                recv_sem=ret_rs.at[1, o],
                device_id=(peer, C),
                device_id_type=MESH,
            )
        )
    for o in range(1, COLS):
        peer = col_at(o)
        at = lax.rem(peer, 2) * 8 + lax.div(peer, 2)
        returns[0].append(
            pltpu.make_async_remote_copy(
                src_ref=ysend.at[0, pl.ds(at * 32, 32)],
                dst_ref=yrecv.at[0, kchunk, pl.ds(half * 32, 32)],
                send_sem=ret_ss.at[0, o],
                recv_sem=ret_rs.at[0, o],
                device_id=(R, peer),
                device_id_type=MESH,
            )
        )

    for copy in carries[1]:
        copy.wait_recv()
    ysend[1] = second_pass(1)
    for copy in returns[1]:
        copy.start()
    yrecv[1, R] = ysend[1, pl.ds(R * TOK, TOK), :]

    for copy in carries[0]:
        copy.wait_recv()
    rows_out = second_pass(0)
    for b in range(2):
        ysend[0, b * 256 : (b + 1) * 256, :] = dot(
            perm[1], rows_out[b * 256 : (b + 1) * 256, :]
        ).astype(BF16)
    for copy in returns[0]:
        copy.start()
    yrecv[0, kchunk, pl.ds(half * 32, 32), :] = ysend[0, pl.ds(slot * 32, 32), :]

    for copy in loads[7:]:
        copy.wait()
    gate_in = dot(normed[...], gate_w[...]).astype(BF16).astype(F32)
    gate_silu = silu(gate_in)
    for k in range(KC):
        gate[k] = chunk(gate_silu, k)
    gains = skip[0:1, :] + skip[1:2, :] + skip[2:3, :] + skip[3:4, :]
    skipped = act[...] * gains
    pieces = [chunk(skipped, k) for k in range(KC)]
    for g in (1, 0):
        for copy in returns[g]:
            copy.wait_recv()
    pieces = [
        pieces[k] + yrecv[0, k].astype(F32) + yrecv[1, k].astype(F32) for k in range(KC)
    ]
    average = jnp.sum(sum(pieces), -1, keepdims=True) * (1.0 / HID)
    mask = lane_mask(TOK)
    centred = [jnp.where(mask, z - average, 0.0) for z in pieces]
    variance = jnp.sum(sum(z * z for z in centred), -1, keepdims=True) * (1.0 / HID)
    scale = lax.rsqrt(variance + epsilon)
    result = jnp.zeros((TOK, CH), F32)
    for k in range(KC):
        gated = (centred[k] * scale * gate[k]).astype(BF16)
        result = result + dot(gated[:, :CW], out_w[k * CW : (k + 1) * CW, :])
    out[...] = result.astype(BF16)

    for copy in rim_copies:
        copy.wait_send()
    for g in range(2):
        for group in (a2a[g], carries[g], returns[g]):
            for copy in group:
                copy.wait_send()


def per_device(
    patches,
    in_weight,
    conv_weight,
    proj_weight,
    step_weight,
    step_bias,
    decay_rate,
    skip_gain,
    out_weight,
):
    vmem = pl.BlockSpec(memory_space=pltpu.VMEM)
    dma = pltpu.SemaphoreType.DMA
    result = pl.pallas_call(
        kernel,
        out_shape=jax.ShapeDtypeStruct((TOK, CH), BF16),
        in_specs=[pl.BlockSpec(memory_space=pl.ANY)] * 9,
        out_specs=vmem,
        scratch_shapes=[
            pltpu.VMEM((TOK, CH), BF16),
            pltpu.VMEM((CH, HID), BF16),
            pltpu.VMEM((3, 3, HID), F32),
            pltpu.VMEM((4, RANK + 2 * NS, HID), BF16),
            pltpu.VMEM((4, RANK, HID), BF16),
            pltpu.VMEM((4, HID), F32),
            pltpu.VMEM((4, NS, HID), F32),
            pltpu.VMEM((CH, HID), BF16),
            pltpu.VMEM((4, HID), F32),
            pltpu.VMEM((HID, CH), BF16),
            pltpu.VMEM((32, CH), BF16),
            pltpu.VMEM((128, CH), BF16),
            pltpu.VMEM((TOK + 128, HID), BF16),
            pltpu.VMEM((3, RIM, TOK + 128), BF16),
            pltpu.VMEM((3, RIM, HID), F32),
            pltpu.VMEM((TOK, CH), BF16),
            pltpu.VMEM((KC, TOK, LANE), F32),
            pltpu.VMEM((TOK, HID), F32),
            pltpu.VMEM((2, TOK, LANE), F32),
            pltpu.VMEM((2, KC, TOK, 2 * LANE), BF16),
            pltpu.VMEM((SPAN, 2 * LANE), BF16),
            pltpu.VMEM((2, SPAN, 2 * LANE), BF16),
            pltpu.VMEM((2, LANE, 2 * LANE), F32),
            pltpu.VMEM((2, 8, 2 * LANE), F32),
            pltpu.VMEM((4, MAP, LANE), F32),
            pltpu.VMEM((4, SLOT * 8, LANE), F32),
            pltpu.VMEM((2, 256, 256), BF16),
            pltpu.VMEM((2 * LANE, WIDE), BF16),
            pltpu.VMEM((WIDE, LANE), BF16),
            pltpu.VMEM((SEG, SPAN), BF16),
            pltpu.VMEM((LANE, 4 * BOTH), BF16),
            pltpu.VMEM((4, SPAN, WIDE), F32),
            pltpu.VMEM((4, SPAN, WIDE), F32),
            pltpu.VMEM((2, SPAN, 4 * BOTH), F32),
            pltpu.VMEM((4, MAP * SEG, LANE), F32),
            pltpu.VMEM((4, MAP * SEG, LANE), F32),
            pltpu.VMEM((4, MAP * SEG, LANE), F32),
            pltpu.VMEM((2, 2, MAP, LANE), F32),
            pltpu.VMEM((2, 2, MAP, LANE), BF16),
            pltpu.VMEM((2, PEERS, MAP, LANE), BF16),
            pltpu.VMEM((2, SPAN, WIDE), F32),
            pltpu.VMEM((2, SPAN, LANE), BF16),
            pltpu.VMEM((2, KC, TOK, LANE), BF16),
            dma((10,)),
            dma((8,)),
            dma((8,)),
            dma((2, 16)),
            dma((2, 16)),
            dma((2, 16)),
            dma((2, 16)),
            dma((2, 16)),
            dma((2, 16)),
        ],
        compiler_params=pltpu.CompilerParams(
            collective_id=0, has_side_effects=True, vmem_limit_bytes=63 * 1024 * 1024
        ),
        name="ss2d",
    )(
        patches.reshape(TOK, CH),
        in_weight,
        conv_weight,
        jnp.swapaxes(proj_weight, 1, 2),
        step_weight,
        step_bias,
        decay_rate,
        skip_gain,
        out_weight,
    )
    return result.reshape(TR, TC, CH)


def solution(mesh):
    return jax.shard_map(
        per_device,
        mesh=mesh,
        in_specs=(P("row", "col", None), P(), P(), P(), P(), P(), P(), P(), P()),
        out_specs=P("row", "col", None),
        check_vma=False,
    )
```

```python
import functools

import jax
import jax.numpy as jnp
from jax import lax
from jax.experimental import pallas as pl
from jax.experimental.pallas import tpu as pltpu
from jax.sharding import PartitionSpec as P

MESH = pl.DeviceIdType.MESH
F32, BF16 = jnp.float32, jnp.bfloat16

ROWS, COLS = 8, 16
TR, TC = 4, 16
TOK = TR * TC
RIM = (TR + 2) * TC
CH, HID = 384, 768
RANK, NS = 24, 16
KC = 8
CW = HID // KC
LANE = 128
SECOND = 64
SEG, POS = 16, 32
GROUP = 16
KIND = CW // GROUP
WIDE = KIND * LANE
SLOT = 2 * KIND
BOTH = 2 * LANE
MAP = 16
SPAN = SEG * POS
TURN = 4
PEERS = 16
LOG2E = 1.4426950408889634
epsilon = 1e-05


def normalised(x):
    average = jnp.mean(x, -1, keepdims=True)
    centred = x - average
    variance = jnp.mean(centred * centred, -1, keepdims=True)
    return centred * lax.rsqrt(variance + epsilon)


def silu(v):
    return v / (1.0 + jnp.exp(-v))


def softplus(v):
    return jnp.maximum(v, 0.0) + jnp.log1p(jnp.exp(-jnp.abs(v)))


def dot(a, b):
    return jnp.dot(a, b, preferred_element_type=F32)


def two_parts(x):
    high = x.astype(BF16)
    return jnp.concatenate([high, (x - high.astype(F32)).astype(BF16)], axis=1)


def zero_one(shape, test):
    one = lax.broadcasted_iota(jnp.int32, shape, 0)
    other = lax.broadcasted_iota(jnp.int32, shape, 1)
    return jnp.where(test(one, other), 1.0, 0.0).astype(BF16)


def lane_mask(rows):
    return lax.broadcasted_iota(jnp.int32, (rows, LANE), 1) < CW


def chunk(x, k):
    low = CW * k
    tile, off = low // LANE, low % LANE
    width = min(2 * LANE, HID - tile * LANE)
    window = x[:, tile * LANE : tile * LANE + width]
    if off:
        window = pltpu.roll(window, width - off, 1)
    return jnp.where(lane_mask(x.shape[0]), window[:, :LANE], 0.0)


def kernel(
    patches_any,
    in_w_any,
    conv_w_any,
    proj_w_any,
    step_w_any,
    step_b_any,
    decay_any,
    skip_any,
    out_w_any,
    out,
    patches,
    in_w,
    conv_w,
    proj_w,
    step_w,
    step_b,
    decay,
    gate_w,
    skip,
    out_w,
    halo_send,
    halo_recv,
    cells,
    shift,
    shifted,
    normed,
    gate,
    act,
    proj,
    a2a_send,
    raw,
    tokens,
    sw,
    bias,
    rates,
    rates_wide,
    perm,
    tile,
    fold,
    gather,
    rep,
    step,
    inflow,
    wide,
    ends,
    decays,
    start,
    msg_f32,
    msg,
    cbuf,
    ysum,
    ysend,
    yrecv,
    load_sem,
    halo_ss,
    halo_rs,
    a2a_ss,
    a2a_rs,
    car_ss,
    car_rs,
    ret_ss,
    ret_rs,
):
    R = lax.axis_index("row")
    C = lax.axis_index("col")
    half = lax.rem(C, 2)
    pair = C - half + (1 - half)
    kchunk = lax.div(C, 2)

    barrier = pltpu.get_barrier_semaphore()

    def greet(r, c):
        pl.semaphore_signal(barrier, inc=1, device_id=(r, c), device_id_type=MESH)

    def row_at(o):
        return lax.rem(R + o, ROWS)

    def col_at(o):
        return lax.rem(C + o, COLS)

    for o in range(1, ROWS):
        greet(row_at(o), C)
        greet(row_at(o), pair)
    for o in range(1, COLS):
        greet(R, col_at(o))
    beside = lax.rem(C + 15 + 2 * half, COLS)
    greet(row_at(1), beside)
    greet(row_at(ROWS - 1), beside)

    loads = [
        pltpu.make_async_copy(source, target, load_sem.at[i])
        for i, (source, target) in enumerate(
            (
                (patches_any, patches),
                (in_w_any.at[:, pl.ds(0, HID)], in_w),
                (conv_w_any, conv_w),
                (proj_w_any, proj_w),
                (step_w_any, step_w),
                (step_b_any, step_b),
                (decay_any, decay),
                (in_w_any.at[:, pl.ds(HID, HID)], gate_w),
                (skip_any, skip),
                (out_w_any, out_w),
            )
        )
    ]
    for copy in loads:
        copy.start()

    picks = zero_one(
        (32, TOK),
        lambda i, t: (t == jnp.where(i < 16, i * TC + TC - 1, (i - 16) * TC))
        & (lax.rem(i, 16) < TR),
    )
    loads[0].wait()
    x = patches[...]
    halo_send[...] = dot(picks, x).astype(BF16)
    pl.semaphore_wait(barrier, 15 + 7 + 7 + 2)

    top, bottom = patches.at[pl.ds(0, 16)], patches.at[pl.ds(TOK - 16, 16)]
    right_edge, left_edge = halo_send.at[pl.ds(0, 16)], halo_send.at[pl.ds(16, 16)]
    rim = (
        (bottom, 1, 0),
        (top, 7, 0),
        (right_edge, 0, 1),
        (left_edge, 0, 15),
        (bottom, 1, 1),
        (bottom, 1, 15),
        (top, 7, 1),
        (top, 7, 15),
    )
    rim_copies = []
    for slot, (edge, dr, dc) in enumerate(rim):
        rim_copies.append(
            pltpu.make_async_remote_copy(
                src_ref=edge,
                dst_ref=halo_recv.at[pl.ds(slot * 16, 16)],
                send_sem=halo_ss.at[slot],
                recv_sem=halo_rs.at[slot],
                device_id=(row_at(dr), col_at(dc)),
                device_id_type=MESH,
            )
        )
    for copy in rim_copies:
        copy.start()

    loads[1].wait()
    normed[...] = normalised(x.astype(F32)).astype(BF16)
    cells[:TOK, :] = dot(normed[...], in_w[...]).astype(BF16)
    for q in range(3):

        def from_cell(i, j):
            r, c = lax.div(i, TC) - 1, lax.rem(i, TC) + (q - 1)
            above, below, left, right = r < 0, r >= TR, c < 0, c >= TC
            source = jnp.where(above, c, jnp.where(below, TC + c, 0)) + TOK
            source = jnp.where(above | below, source, r * TC + c)
            side = jnp.where(
                above,
                jnp.where(left, 79, 80),
                jnp.where(below, jnp.where(left, 111, 112), jnp.where(left, 32, 48) + r),
            )
            source = jnp.where(left | right, side + TOK, source)
            outside = (above & (R == 0)) | (below & (R == ROWS - 1))
            outside = outside | (left & (C == 0)) | (right & (C == COLS - 1))
            return (j == source) & jnp.logical_not(outside)

        shift[q] = zero_one((RIM, TOK + 128), from_cell)

    for slot in range(8):
        rim_copies[slot].wait_recv()
    cells[TOK:, :] = dot(
        normalised(halo_recv[...].astype(F32)).astype(BF16), in_w[...]
    ).astype(BF16)
    for q in range(3):
        shifted[q] = dot(shift[q], cells[...])
    loads[2].wait()
    for i in range(TR):
        total = jnp.zeros((TC, HID), F32)
        for p in range(3):
            for q in range(3):
                total = total + shifted[q, (i + p) * TC : (i + p + 1) * TC, :] * conv_w[p, q : q + 1, :]
        act[i * TC : (i + 1) * TC, :] = silu(total).astype(BF16).astype(F32)

    activated = act[...]
    low = activated.astype(BF16)
    proj[...] = jnp.zeros_like(proj)
    loads[3].wait()
    for branch in range(4):
        g, d = branch % 2, branch // 2
        proj[g, :, d * SECOND : d * SECOND + RANK + 2 * NS] = lax.dot_general(
            low, proj_w[branch], (((1,), (1,)), ((), ())), preferred_element_type=F32
        )
    for k in range(KC):
        part_k = chunk(activated, k).astype(BF16)
        for g in range(2):
            a2a_send[g, k, :, :LANE] = part_k
            a2a_send[g, k, :, LANE:] = proj[g].astype(BF16)

    a2a = {0: [], 1: []}
    for o in range(1, ROWS):
        peer = row_at(o)
        a2a[1].append(
            pltpu.make_async_remote_copy(
                src_ref=a2a_send.at[1, peer],
                dst_ref=tokens.at[1, pl.ds(R * TOK, TOK)],
                send_sem=a2a_ss.at[1, o],
                recv_sem=a2a_rs.at[1, o],
                device_id=(peer, C),
                device_id_type=MESH,
            )
        )
    slot = half * 8 + kchunk
    for o in range(1, COLS):
        peer = col_at(o)
        a2a[0].append(
            pltpu.make_async_remote_copy(
                src_ref=a2a_send.at[0, lax.div(peer, 2), pl.ds(lax.rem(peer, 2) * 32, 32)],
                dst_ref=raw.at[pl.ds(slot * 32, 32)],
                send_sem=a2a_ss.at[0, o],
                recv_sem=a2a_rs.at[0, o],
                device_id=(R, peer),
                device_id_type=MESH,
            )
        )
    for copy in a2a[0]:
        copy.start()
    tokens[1, pl.ds(R * TOK, TOK), :] = a2a_send[1, R]
    raw[pl.ds(slot * 32, 32), :] = a2a_send[0, kchunk, pl.ds(half * 32, 32), :]

    def arrival(p):
        return lax.rem(p, 8) * 32 + lax.rem(lax.div(p, 8), 2) * 16 + lax.div(p, 16)

    perm[0] = zero_one((256, 256), lambda i, j: j == arrival(i))
    perm[1] = zero_one((256, 256), lambda i, j: i == arrival(j))

    def channel(j):
        return lax.div(j, LANE) * GROUP + lax.rem(j, GROUP)

    tile[...] = zero_one((2 * LANE, WIDE), lambda i, j: lax.rem(i, LANE) == channel(j))
    fold[...] = zero_one((WIDE, LANE), lambda i, j: channel(i) == j)
    gather[...] = zero_one((SEG, SPAN), lambda i, j: i == lax.rem(j, SEG))
    for d in range(2):
        for i in range(2):
            first = d * SECOND + RANK + i * NS
            at = (2 * d + i) * BOTH
            rep[:, at : at + BOTH] = zero_one(
                (LANE, BOTH), lambda k, j: k - first == lax.div(j, GROUP)
            )

    for copy in loads[4:7]:
        copy.wait()
    sw[...] = jnp.zeros_like(sw)
    wide_lane = lax.broadcasted_iota(jnp.int32, (NS, WIDE), 1)
    wide_n = lax.broadcasted_iota(jnp.int32, (NS, WIDE), 0)
    own_lanes = lax.div(lax.rem(wide_lane, LANE), GROUP) == lax.rem(wide_n, 8)
    for g in range(2):
        turn = lax.rem(HID - CW * (kchunk if g == 0 else R), HID)
        for d in range(2):
            branch = g + 2 * d

            def part(value):
                turned = pltpu.roll(value, turn, 1)[:, :LANE]
                return jnp.where(lane_mask(value.shape[0]), turned, 0.0)

            sw[g, d * SECOND : d * SECOND + RANK, d * LANE : (d + 1) * LANE] = part(
                step_w[branch].astype(F32)
            )
            bias[g, :, d * LANE : (d + 1) * LANE] = part(
                jnp.broadcast_to(step_b[branch : branch + 1, :], (8, HID))
            )
            spread = dot(two_parts(part(decay[branch]) * (-LOG2E)), tile[...])
            spread = jnp.where(own_lanes, spread, 0.0)
            b = 2 * g + d
            rates[b] = jnp.zeros((MAP, LANE), F32)
            for m in range(2):
                eight = jnp.sum(spread[8 * m : 8 * m + 8], 0, keepdims=True)
                for kind in range(KIND):
                    j = m * KIND + kind
                    one = eight[:, kind * LANE : (kind + 1) * LANE]
                    rates[b, j : j + 1, :] = one
                    rates_wide[b, j * 8 : (j + 1) * 8, :] = jnp.broadcast_to(
                        one, (8, LANE)
                    )
            ends[b, SLOT * SEG :, :] = jnp.zeros(((MAP - SLOT) * SEG, LANE), F32)
            decays[b, SLOT * SEG :, :] = jnp.zeros(((MAP - SLOT) * SEG, LANE), F32)
    place = (R * 2 + half, C)
    for g in range(2):
        cbuf[g, place[g]] = jnp.zeros((MAP, LANE), BF16)

    for copy in a2a[1]:
        copy.start()

    def peer_of(g, s):
        if g == 0:
            return (lax.div(s, 2), C - half + lax.rem(s, 2))
        return (R, s)

    carries = {0: [], 1: []}
    for g in range(2):
        for o in range(1, PEERS):
            s = lax.rem(place[g] + o, PEERS)
            way = jnp.where(s > place[g], 0, 1)
            carries[g].append(
                pltpu.make_async_remote_copy(
                    src_ref=msg.at[g, way],
                    dst_ref=cbuf.at[g, place[g]],
                    send_sem=car_ss.at[g, o],
                    recv_sem=car_rs.at[g, o],
                    device_id=peer_of(g, s),
                    device_id_type=MESH,
                )
            )

    def scan(b, hf, backward, with_output):
        g, d = b // 2, b % 2
        rate = [rates_wide[b, j * 8 : (j + 1) * 8, :] for j in range(SLOT)]

        def body(i, held):
            for u in range(TURN):
                pos = i * TURN + u
                pos = POS - 1 - pos if backward else pos
                rows = pl.ds(pl.multiple_of(pos * SEG + hf * 8, 8), 8)

                def part(ref, at, k):
                    return ref[at, rows, k * LANE : (k + 1) * LANE]

                st = [part(step, b, k) for k in range(KIND)]
                fl = [part(inflow, b, k) for k in range(KIND)]
                w = [part(wide, g, 4 * d + m) for m in range(2)]
                r = [part(wide, g, 4 * d + 2 + m) for m in range(2)] if with_output else None
                new, outs = [], [None] * KIND
                for j in range(SLOT):
                    m, k = j // KIND, j % KIND
                    h = jnp.exp2(st[k] * rate[j]) * held[j] + fl[k] * w[m]
                    new.append(h)
                    if with_output:
                        y = h * r[m]
                        outs[k] = y if outs[k] is None else outs[k] + y
                held = tuple(new)
                if with_output:
                    for k in range(KIND):
                        y = outs[k] + part(ysum, g, k) if d == 1 else outs[k]
                        ysum[g, rows, k * LANE : (k + 1) * LANE] = y
            return held

        if with_output:
            first = tuple(
                start[b, j * SEG + hf * 8 : j * SEG + hf * 8 + 8, :] for j in range(SLOT)
            )
            lax.fori_loop(0, POS // TURN, body, first)
            return
        zero = jnp.zeros((8, LANE), F32)
        held = lax.fori_loop(0, POS // TURN, body, (zero,) * SLOT)
        for j in range(SLOT):
            ends[b, j * SEG + hf * 8 : j * SEG + hf * 8 + 8, :] = held[j]

    def in_order(d, count):
        return range(count - 1, -1, -1) if d == 1 else range(count)

    def first_pass(g):
        packed = tokens[g, :, LANE:]
        signal = dot(tokens[g, :, :LANE], tile[:LANE, :])
        steps = softplus(dot(packed, sw[g].astype(BF16)) + bias[g, 0:1, :])
        wide[g] = dot(packed, rep[...])
        for d in range(2):
            b = 2 * g + d
            parts = two_parts(steps[:, d * LANE : (d + 1) * LANE])
            step[b] = dot(parts, tile[...])
            inflow[b] = step[b] * signal
            sums = dot(gather[...], parts)
            sums = sums[:, :LANE] + sums[:, LANE:]
            of_lanes = dot(two_parts(sums), tile[...])
            for j in range(SLOT):
                k = j % KIND
                decays[b, j * SEG : (j + 1) * SEG, :] = jnp.exp2(
                    of_lanes[:, k * LANE : (k + 1) * LANE] * rates[b, j : j + 1, :]
                )
            total = jnp.sum(sums, 0, keepdims=True)
            msg_f32[g, d] = jnp.zeros((MAP, LANE), F32)
            for i in range(3):
                piece = total.astype(BF16).astype(F32)
                msg_f32[g, d, SLOT + i : SLOT + i + 1, :] = piece
                total = total - piece
        for d in range(2):
            b = 2 * g + d
            for hf in range(2):
                scan(b, hf, d == 1, False)
            held = jnp.zeros((MAP, LANE), F32)
            for seg in in_order(d, SEG):
                held = (
                    decays[b, pl.ds(seg, MAP, stride=SEG), :] * held
                    + ends[b, pl.ds(seg, MAP, stride=SEG), :]
                )
            msg_f32[g, d, :SLOT, :] = held[:SLOT]
            msg[g, d] = msg_f32[g, d].astype(BF16)
        for copy in carries[g]:
            copy.start()

    def second_pass(g):
        maps = cbuf[g].reshape(PEERS * MAP, LANE)
        sums = dot(maps, tile[:LANE, :])
        kind = lax.rem(lax.broadcasted_iota(jnp.int32, (MAP, LANE), 0), KIND)
        factors = []
        for s in range(PEERS):
            at = s * MAP + SLOT
            total = sums[at : at + 1] + sums[at + 1 : at + 2] + sums[at + 2 : at + 3]
            of_slot = total[:, :LANE]
            for k in range(1, KIND):
                of_slot = jnp.where(kind == k, total[:, k * LANE : (k + 1) * LANE], of_slot)
            factors.append(
                jnp.exp2(of_slot * jnp.where(s < place[g], rates[2 * g], rates[2 * g + 1]))
            )
        for d in range(2):
            b = 2 * g + d
            held = jnp.zeros((MAP, LANE), F32)
            for s in in_order(d, PEERS):
                ahead = s > place[g] if d == 1 else s < place[g]
                later = factors[s] * held + cbuf[g, s].astype(F32)
                held = jnp.where(ahead, later, held)
            for seg in in_order(d, SEG):
                start[b, pl.ds(seg, MAP, stride=SEG), :] = held
                held = (
                    decays[b, pl.ds(seg, MAP, stride=SEG), :] * held
                    + ends[b, pl.ds(seg, MAP, stride=SEG), :]
                )
            for hf in range(2):
                scan(b, hf, d == 1, True)
        return dot(ysum[g].astype(BF16), fold[...]).astype(BF16)

    for copy in a2a[0]:
        copy.wait_recv()
    for b in range(2):
        tokens[0, b * 256 : (b + 1) * 256, :] = dot(
            perm[0], raw[b * 256 : (b + 1) * 256, :]
        ).astype(BF16)
    first_pass(0)
    for copy in a2a[1]:
        copy.wait_recv()
    first_pass(1)
    returns = {0: [], 1: []}
    for o in range(1, ROWS):
        peer = row_at(o)
        returns[1].append(
            pltpu.make_async_remote_copy(
                src_ref=ysend.at[1, pl.ds(peer * TOK, TOK)],
                dst_ref=yrecv.at[1, R],
                send_sem=ret_ss.at[1, o],
                recv_sem=ret_rs.at[1, o],
                device_id=(peer, C),
                device_id_type=MESH,
            )
        )
    for o in range(1, COLS):
        peer = col_at(o)
        at = lax.rem(peer, 2) * 8 + lax.div(peer, 2)
        returns[0].append(
            pltpu.make_async_remote_copy(
                src_ref=ysend.at[0, pl.ds(at * 32, 32)],
                dst_ref=yrecv.at[0, kchunk, pl.ds(half * 32, 32)],
                send_sem=ret_ss.at[0, o],
                recv_sem=ret_rs.at[0, o],
                device_id=(R, peer),
                device_id_type=MESH,
            )
        )

    for copy in carries[0]:
        copy.wait_recv()
    rows_out = second_pass(0)
    for b in range(2):
        ysend[0, b * 256 : (b + 1) * 256, :] = dot(
            perm[1], rows_out[b * 256 : (b + 1) * 256, :]
        ).astype(BF16)
    for copy in returns[0]:
        copy.start()
    yrecv[0, kchunk, pl.ds(half * 32, 32), :] = ysend[0, pl.ds(slot * 32, 32), :]

    for copy in carries[1]:
        copy.wait_recv()
    ysend[1] = second_pass(1)
    for copy in returns[1]:
        copy.start()
    yrecv[1, R] = ysend[1, pl.ds(R * TOK, TOK), :]

    for copy in loads[7:]:
        copy.wait()
    gate_in = dot(normed[...], gate_w[...]).astype(BF16).astype(F32)
    gate_silu = silu(gate_in)
    for k in range(KC):
        gate[k] = chunk(gate_silu, k)
    gains = skip[0:1, :] + skip[1:2, :] + skip[2:3, :] + skip[3:4, :]
    skipped = act[...] * gains
    pieces = [chunk(skipped, k) for k in range(KC)]
    for g in (0, 1):
        for copy in returns[g]:
            copy.wait_recv()
    pieces = [
        pieces[k] + yrecv[0, k].astype(F32) + yrecv[1, k].astype(F32) for k in range(KC)
    ]
    average = jnp.sum(sum(pieces), -1, keepdims=True) * (1.0 / HID)
    mask = lane_mask(TOK)
    centred = [jnp.where(mask, z - average, 0.0) for z in pieces]
    variance = jnp.sum(sum(z * z for z in centred), -1, keepdims=True) * (1.0 / HID)
    scale = lax.rsqrt(variance + epsilon)
    result = jnp.zeros((TOK, CH), F32)
    for k in range(KC):
        gated = (centred[k] * scale * gate[k]).astype(BF16)
        result = result + dot(gated[:, :CW], out_w[k * CW : (k + 1) * CW, :])
    out[...] = result.astype(BF16)

    for copy in rim_copies:
        copy.wait_send()
    for g in range(2):
        for group in (a2a[g], carries[g], returns[g]):
            for copy in group:
                copy.wait_send()


def per_device(
    patches,
    in_weight,
    conv_weight,
    proj_weight,
    step_weight,
    step_bias,
    decay_rate,
    skip_gain,
    out_weight,
):
    vmem = pl.BlockSpec(memory_space=pltpu.VMEM)
    dma = pltpu.SemaphoreType.DMA
    result = pl.pallas_call(
        kernel,
        out_shape=jax.ShapeDtypeStruct((TOK, CH), BF16),
        in_specs=[pl.BlockSpec(memory_space=pl.ANY)] * 9,
        out_specs=vmem,
        scratch_shapes=[
            pltpu.VMEM((TOK, CH), BF16),
            pltpu.VMEM((CH, HID), BF16),
            pltpu.VMEM((3, 3, HID), F32),
            pltpu.VMEM((4, RANK + 2 * NS, HID), BF16),
            pltpu.VMEM((4, RANK, HID), BF16),
            pltpu.VMEM((4, HID), F32),
            pltpu.VMEM((4, NS, HID), F32),
            pltpu.VMEM((CH, HID), BF16),
            pltpu.VMEM((4, HID), F32),
            pltpu.VMEM((HID, CH), BF16),
            pltpu.VMEM((32, CH), BF16),
            pltpu.VMEM((128, CH), BF16),
            pltpu.VMEM((TOK + 128, HID), BF16),
            pltpu.VMEM((3, RIM, TOK + 128), BF16),
            pltpu.VMEM((3, RIM, HID), F32),
            pltpu.VMEM((TOK, CH), BF16),
            pltpu.VMEM((KC, TOK, LANE), F32),
            pltpu.VMEM((TOK, HID), F32),
            pltpu.VMEM((2, TOK, LANE), F32),
            pltpu.VMEM((2, KC, TOK, 2 * LANE), BF16),
            pltpu.VMEM((SPAN, 2 * LANE), BF16),
            pltpu.VMEM((2, SPAN, 2 * LANE), BF16),
            pltpu.VMEM((2, LANE, 2 * LANE), F32),
            pltpu.VMEM((2, 8, 2 * LANE), F32),
            pltpu.VMEM((4, MAP, LANE), F32),
            pltpu.VMEM((4, SLOT * 8, LANE), F32),
            pltpu.VMEM((2, 256, 256), BF16),
            pltpu.VMEM((2 * LANE, WIDE), BF16),
            pltpu.VMEM((WIDE, LANE), BF16),
            pltpu.VMEM((SEG, SPAN), BF16),
            pltpu.VMEM((LANE, 4 * BOTH), BF16),
            pltpu.VMEM((4, SPAN, WIDE), F32),
            pltpu.VMEM((4, SPAN, WIDE), F32),
            pltpu.VMEM((2, SPAN, 4 * BOTH), F32),
            pltpu.VMEM((4, MAP * SEG, LANE), F32),
            pltpu.VMEM((4, MAP * SEG, LANE), F32),
            pltpu.VMEM((4, MAP * SEG, LANE), F32),
            pltpu.VMEM((2, 2, MAP, LANE), F32),
            pltpu.VMEM((2, 2, MAP, LANE), BF16),
            pltpu.VMEM((2, PEERS, MAP, LANE), BF16),
            pltpu.VMEM((2, SPAN, WIDE), F32),
            pltpu.VMEM((2, SPAN, LANE), BF16),
            pltpu.VMEM((2, KC, TOK, LANE), BF16),
            dma((10,)),
            dma((8,)),
            dma((8,)),
            dma((2, 16)),
            dma((2, 16)),
            dma((2, 16)),
            dma((2, 16)),
            dma((2, 16)),
            dma((2, 16)),
        ],
        compiler_params=pltpu.CompilerParams(
            collective_id=0, has_side_effects=True, vmem_limit_bytes=63 * 1024 * 1024
        ),
        name="ss2d",
    )(
        patches.reshape(TOK, CH),
        in_weight,
        conv_weight,
        jnp.swapaxes(proj_weight, 1, 2),
        step_weight,
        step_bias,
        decay_rate,
        skip_gain,
        out_weight,
    )
    return result.reshape(TR, TC, CH)


def solution(mesh):
    return jax.shard_map(
        per_device,
        mesh=mesh,
        in_specs=(P("row", "col", None), P(), P(), P(), P(), P(), P(), P(), P()),
        out_specs=P("row", "col", None),
        check_vma=False,
    )
```
